512 devices in a mesh: replica: 64 (over x, z), tensor: 8 (over y, core).
Axes of the slice: x: 4, y: 4, z: 16, core: 2. Of those that a mesh axis runs over, the one named last changes fastest.
Arguments:
- suffix_x: bfloat16 [16384, 8192], P('replica', 'tensor'), may hold values from -6 to 6
- suffix_z: bfloat16 [16384, 8192], P('replica', 'tensor'), may hold values from -6 to 6
- suffix_b: bfloat16 [16384, 2048], P('replica', 'tensor'), may hold values from -1.5 to 1.5
- suffix_c: bfloat16 [16384, 2048], P('replica', 'tensor'), may hold values from -1.5 to 1.5
- suffix_dt: float32 [16384, 128], P('replica', 'tensor'), may hold values from -3 to 15
- missed_x: bfloat16 [49152, 8192], P('replica', 'tensor'), may hold values from -6 to 6
- missed_b: bfloat16 [49152, 2048], P('replica', 'tensor'), may hold values from -1.5 to 1.5
- missed_dt: float32 [49152, 128], P('replica', 'tensor'), may hold values from -3 to 15
- dt_bias: float32 [128], P('tensor'), may hold values from -1 to 1
- a_log: float32 [128], P('tensor'), may hold values from -8 to -2
- skip_weight_per_head: float32 [128], P('tensor'), may hold values from 0.5 to 2
- norm_gain: float32 [8192], P('tensor'), may hold values from 0.1 to 1.9
- out_weight: bfloat16 [8192, 4096], P('tensor', 'replica'), may hold values from -0.1875 to 0.1875
- cache_pages: bfloat16 [3072, 8, 32, 256], P('replica', 'tensor'), may hold values from -12 to 12
- hit_holder: int32 [8, 128, 32, 1], P('tensor'), may hold values from 0 to 63; in each aligned block of 64 rows (0 to 63, 64 to 127, ..., all dimensions but the last counted through in order) at most 2 rows name the same one
- hit_slot: int32 [8, 128, 32], P('tensor'), may hold values from 0 to 47
- missed: int32 [128], P('replica'), may hold values from 0 to 3, as said below
Outputs:
- mixed: bfloat16 [16384, 4096], P('replica', 'tensor')
The draws below stay inside these ranges and needn't reach their ends.
Inputs may be any that keep to these rules, and one draw needn't show every extreme that they name: `hit_holder`: among the pages of the 2 requests r * 2 .. r * 2 + 1 in one set of heads, at most 2 name the same holder, and in each draw some holder is named by exactly 2 of them. `missed`: some request misses all 3 blocks in every draw.
All inputs are finite; a program needn't handle non-finite values.
Results may differ from the reference program's by a relative error of at most 0.017.
Values may be sent and summed in bfloat16 or wider, within the bound.
A program may use at most 64 MiB of HBM per device.

```python
import math
import jax
import jax.numpy as jnp
import numpy as np
from jax import lax

D = 4096
HEADS = 128
P_SIZE = 64
N = 256
GROUPS = 8
SPAN = 128
REQ_DEV = 2
MISS_MAX = 3
SLOTS = 48
PAGE_ROWS = 32
HEAD_SETS = 8
PAGES_REQ = 32
CAP = 2
REQUESTS = 128
TOKENS = 16384
MISSED_TOKENS = 49152
PAGES_ALL = 3072
N_REPLICA = 64
N_TENSOR = 8


def spike_step_count(key, reference_level):
    spike_events = jax.random.bernoulli(jax.random.fold_in(key, 5), 0.01, reference_level.shape)
    return reference_level + jnp.where(spike_events, 12.0, 0.0)


def draw_suffix_dt(key, part):
    key = jax.random.fold_in(key, 11)
    reference_level = jnp.clip(0.5 * jax.random.normal(jax.random.fold_in(key, 1), (TOKENS, HEADS), jnp.float32), -3.0, 3.0)
    return spike_step_count(key, reference_level)


def draw_missed_dt(key, part):
    key = jax.random.fold_in(key, 12)
    reference_level = jnp.clip(0.5 * jax.random.normal(jax.random.fold_in(key, 1), (MISSED_TOKENS, HEADS), jnp.float32), -3.0, 3.0)
    return spike_step_count(key, reference_level)


def draw_a_log(key, part):
    key = jax.random.fold_in(key, 13)
    return jax.random.uniform(key, (HEADS,), jnp.float32, -6.9, -3.0)


def draw_missed(key, part):
    key = jax.random.fold_in(key, 17)
    counts = jax.random.randint(key, (REQUESTS,), 0, MISS_MAX + 1)
    fullest = jax.random.randint(jax.random.fold_in(key, 1), (), 0, REQUESTS)
    return counts.at[fullest].set(MISS_MAX)


def touch_ends(drawn, stream_key, smallest, high):
    longest = drawn.shape.index(max(drawn.shape))
    spots = []
    for shift in (0, 1):
        where = [jax.random.randint(jax.random.fold_in(stream_key, axis), (), 0, length) for axis, length in enumerate(drawn.shape)]
        where[longest] = (where[longest] + shift) % drawn.shape[longest]
        spots.append(tuple(where))
    return drawn.at[spots[0]].set(smallest).at[spots[1]].set(high)


def spiked(drawn, rng, source, target, blocks, factor):
    owner, partner = [(jnp.arange(drawn.shape[dim]) // (drawn.shape[dim] // blocks)).reshape([-1 if axis == dim else 1 for axis in range(drawn.ndim)]) for dim in (source, target)]
    chosen = jax.random.permutation(rng, blocks)[partner]
    strong = (owner == chosen) | (owner == (partner + blocks // 2) % blocks)
    return jnp.where(strong, factor * drawn, drawn)


def levels(own_key, shape, cuts, least, high):
    def one(dim, parts):
        heights = jax.random.uniform(jax.random.fold_in(jax.random.fold_in(own_key, 6), dim), (parts,), jnp.float32, least / len(cuts), high / len(cuts))
        return jnp.repeat(jnp.exp(heights), shape[dim] // parts).reshape((-1,) + (1,) * (len(shape) - dim - 1))

    level = one(*cuts[0])
    for cut in cuts[1:]:
        level = level * one(*cut)
    return level


def routed_block(stream_key, own, number, rows, amount, top, reach, slope):
    order = jax.random.permutation(stream_key, amount)
    crowded, ordinary = portions_of(amount, rows * top, reach, slope, True), portions_of(amount, rows * top, reach, slope, False)
    places = jnp.arange(amount)

    def named(tallies, offset_by):
        used = int((tallies > 0).sum())
        fixed = max(1, used // 4)
        shifted = fixed + (places - fixed + offset_by * (used - fixed)) % max(1, amount - fixed)
        return jnp.zeros((amount,), jnp.int32).at[order[jnp.where(places < fixed, places, shifted)]].set(jnp.asarray(tallies, jnp.int32))

    tallies = jnp.where(number % 4 == 0, named(crowded, number // 4), named(ordinary, number - number // 4 - 1))
    mixed = jax.random.permutation(jax.random.fold_in(own, 3), amount)
    source_of, taker = mixed[0:amount // 2 * 2:2], mixed[1:amount // 2 * 2:2]
    room = jnp.minimum(tallies[source_of] - 1, reach - tallies[taker]) // 2
    room = jnp.where((source_of == order[0]) | (taker == order[0]) | (tallies[taker] == 0), 0, jnp.maximum(room, 0))
    shifted = jax.random.randint(jax.random.fold_in(own, 4), (amount // 2,), 0, 1 << 20) % (room + 1)
    tallies = tallies.at[source_of].add(-shifted).at[taker].add(shifted)
    members = jnp.searchsorted(jnp.cumsum(tallies), jnp.arange(rows * top), side="right").astype(jnp.int32)
    listing = members.reshape(top, rows).T
    listing = listing[jax.random.permutation(jax.random.fold_in(own, 1), rows)]
    offset_by = jax.random.randint(jax.random.fold_in(own, 2), (rows, 1), 0, top)
    return jnp.take_along_axis(listing, (jnp.arange(top)[None, :] + offset_by) % top, axis=1)


def portions_of(number_of, total, limit, slope, full):
    portions = [(1 << 20) // math.isqrt(standing ** slope) + 1 for standing in range(1, number_of + 1)]
    largest = limit if full else min(limit, max(-(-total // number_of), total * portions[0] // sum(portions)))
    least = 1 if total - largest >= number_of - 1 else 0
    given, rest = [largest] + [least] * (number_of - 1), total - largest - least * (number_of - 1)
    while rest > 0:
        movable = [i for i in range(1, number_of) if given[i] < largest] or [i for i in range(1, number_of) if given[i] < limit]
        mass, remaining = sum([portions[i] for i in movable]), rest
        for i in movable:
            extra = min(limit - given[i], max(1, remaining * portions[i] // mass), rest)
            given[i] = given[i] + extra
            rest = rest - extra
    return np.array(given)


def bell_draw(stream_key, shape, deviation, bound, pieces=(), kind=jnp.bfloat16):
    level = levels(stream_key, shape, pieces, -0.22, 0.18) if pieces else 1.0
    array = jax.random.normal(stream_key, shape, jnp.float32) * deviation * level
    return jnp.minimum(jnp.maximum(array, -bound), bound).astype(kind)


def heavy_noise(stream_key, extent, width, most, shards, heavy, kind=jnp.bfloat16):
    entries = width * jax.random.normal(stream_key, extent, jnp.float32)
    if shards:
        entries = entries * levels(stream_key, extent, shards, -0.22, 0.18)
    return jnp.clip(spiked(entries, jax.random.fold_in(stream_key, 3), *heavy), -most, most).astype(kind)


def setup_inputs(seed: int = 0) -> dict:
    streams_of = jax.random.split(jax.random.key(seed), 18)
    suffix_x = bell_draw(streams_of[0], (TOKENS, HEADS * P_SIZE), 1.0, 6.0, ((0, 64), (1, 8)))
    suffix_z = bell_draw(streams_of[1], (TOKENS, HEADS * P_SIZE), 1.0, 6.0, ((0, 64), (1, 8)))
    suffix_b = bell_draw(streams_of[2], (TOKENS, GROUPS * N), 0.25, 1.5, ((0, 64), (1, 8)))
    suffix_c = bell_draw(streams_of[3], (TOKENS, GROUPS * N), 0.25, 1.5, ((0, 64), (1, 8)))
    suffix_dt = draw_suffix_dt(jax.random.fold_in(streams_of[17], 71), 0)
    missed_x = bell_draw(streams_of[5], (MISSED_TOKENS, HEADS * P_SIZE), 1.0, 6.0, ((0, 64), (1, 8)))
    missed_b = bell_draw(streams_of[6], (MISSED_TOKENS, GROUPS * N), 0.25, 1.5, ((0, 64), (1, 8)))
    missed_dt = draw_missed_dt(jax.random.fold_in(streams_of[17], 71), 0)
    dt_bias = jnp.clip(jax.random.uniform(streams_of[8], (HEADS,), jnp.float32, -1.0, 1.0) * levels(streams_of[8], (HEADS,), ((0, 8),), -0.4, 0.0), -1.0, 1.0)
    a_log = draw_a_log(jax.random.fold_in(streams_of[17], 71), 0)
    skip_weight_per_head = jnp.clip(0.5 + 1.5 * jax.random.uniform(streams_of[10], (HEADS,), jnp.float32) ** levels(streams_of[10], (HEADS,), ((0, 8),), -0.2, 0.2), 0.5, 2.0)
    norm_gain = jnp.clip(1.0 + 0.18 * jax.random.normal(streams_of[11], (HEADS * P_SIZE,), jnp.float32), 0.1, 1.9)
    out_weight = heavy_noise(streams_of[12], (HEADS * P_SIZE, D), (HEADS * P_SIZE) ** -0.5, 0.1875, ((0, 8), (1, 64)), (0, 1, 64, 4.0))
    cache_pages = bell_draw(streams_of[13], (PAGES_ALL, HEAD_SETS, PAGE_ROWS, N), 2.0, 12.0, ((0, 64), (1, 8)))
    hit_holder_keys = jax.random.split(jax.random.fold_in(streams_of[14], 1), HEAD_SETS * REQUESTS * PAGES_REQ // (REQ_DEV * PAGES_REQ))
    hit_holder_turns = jax.random.permutation(jax.random.fold_in(streams_of[14], 3), HEAD_SETS * REQUESTS * PAGES_REQ // (REQ_DEV * PAGES_REQ))
    hit_holder = jax.vmap(lambda own, number: routed_block(jax.random.fold_in(streams_of[14], 2), own, number, REQ_DEV * PAGES_REQ, N_REPLICA, 1, CAP, 2))(hit_holder_keys, hit_holder_turns).reshape((HEAD_SETS, REQUESTS, PAGES_REQ, 1))
    hit_slot = touch_ends(jax.random.randint(streams_of[15], (HEAD_SETS, REQUESTS, PAGES_REQ), 0, SLOTS), jax.random.fold_in(streams_of[15], 1), 0, SLOTS - 1).astype(jnp.int32)
    missed = draw_missed(jax.random.fold_in(streams_of[17], 71), 0)
    return {"suffix_x": suffix_x, "suffix_z": suffix_z, "suffix_b": suffix_b, "suffix_c": suffix_c, "suffix_dt": suffix_dt, "missed_x": missed_x, "missed_b": missed_b, "missed_dt": missed_dt, "dt_bias": dt_bias, "a_log": a_log, "skip_weight_per_head": skip_weight_per_head, "norm_gain": norm_gain, "out_weight": out_weight, "cache_pages": cache_pages, "hit_holder": hit_holder, "hit_slot": hit_slot, "missed": missed}


def state_update(span_x, span_b, step_size, log_decay, prior):
    length, head_count, head_width = span_x.shape
    groups = span_b.shape[1]
    cumulative = jnp.cumsum(log_decay, axis=0)
    span_total = cumulative[-1]
    weight_matrix = jnp.exp(span_total[None, :] - cumulative) * step_size
    scaled = (span_x.astype(jnp.float32) * weight_matrix[:, :, None]).astype(jnp.bfloat16)
    scaled = lax.optimization_barrier(scaled).astype(jnp.float32)
    scaled = scaled.reshape(length, groups, head_count // groups, head_width)
    gained = jnp.einsum('lgkp,lgn->gkpn', scaled, span_b.astype(jnp.float32))
    return jnp.exp(span_total)[:, None, None] * prior + gained.reshape(head_count, head_width, -1)

def span_output(span_x, span_b, span_c, step_size, log_decay, prior, skip_weight_per_head):
    length, head_count, head_width = span_x.shape
    groups = span_b.shape[1]
    per_group = head_count // groups
    cumulative = jnp.cumsum(log_decay, axis=0)
    scores = jnp.einsum('lgn,sgn->lsg', span_c.astype(jnp.float32), span_b.astype(jnp.float32))
    positions = jnp.arange(length)
    causal = positions[:, None] >= positions[None, :]
    logarithmic_spacing = jnp.where(causal[:, :, None], cumulative[:, None, :] - cumulative[None, :, :], -jnp.inf)
    mixing = jnp.exp(logarithmic_spacing) * step_size[None, :, :]
    mixing = (mixing.reshape(length, length, groups, per_group) * scores[:, :, :, None]).astype(jnp.bfloat16)
    mixing = lax.optimization_barrier(mixing).astype(jnp.float32)
    grouped_x = span_x.reshape(length, groups, per_group, head_width).astype(jnp.float32)
    inner_part = jnp.einsum('lsgk,sgkp->lgkp', mixing, grouped_x)
    carried = jnp.einsum('lgn,gkpn->lgkp', span_c.astype(jnp.float32), prior.reshape(groups, per_group, head_width, -1), precision=lax.Precision.HIGHEST)
    carried = carried * jnp.exp(cumulative).reshape(length, groups, per_group)[:, :, :, None]
    skipped = skip_weight_per_head.reshape(groups, per_group)[:, :, None] * grouped_x
    return (inner_part + carried + skipped).reshape(length, head_count * head_width)

def gate_norm(values, gate_in, norm_scale, groups):
    length = values.shape[0]
    gated = values * jax.nn.silu(gate_in.astype(jnp.float32))
    grouped = gated.reshape(length, groups, -1)
    reciprocal_root_mean = lax.rsqrt(lax.optimization_barrier(jnp.mean(grouped * grouped, axis=-1, keepdims=True)) + 1e-05)
    return ((grouped * reciprocal_root_mean).reshape(length, -1) * norm_scale).astype(jnp.bfloat16)

def reference(suffix_x, suffix_z, suffix_b, suffix_c, suffix_dt, missed_x, missed_b, missed_dt, dt_bias, a_log, skip_weight_per_head, norm_gain, out_weight, cache_pages, hit_holder, hit_slot, missed):
    page_index = (hit_holder[..., 0] * SLOTS + hit_slot).transpose(1, 0, 2)
    set_ids = jnp.arange(N_TENSOR, dtype=jnp.int32)
    decay_rate = -jnp.exp(a_log)

    def one_request(inputs):
        own_x, own_z, own_b, own_c, own_dt, old_x, old_b, old_dt, own_pages, own_missed = inputs
        fetched = cache_pages[own_pages, set_ids[:, None]]
        carried_state = fetched.reshape(HEADS, P_SIZE, N).astype(jnp.float32)
        for position in range(MISS_MAX):
            step_size = jax.nn.softplus(old_dt[position] + dt_bias)
            updated = state_update(old_x[position], old_b[position], step_size, decay_rate * step_size, carried_state)
            carried_state = jnp.where(position >= MISS_MAX - own_missed, updated, carried_state)
        step_size = jax.nn.softplus(own_dt + dt_bias)
        values = span_output(own_x, own_b, own_c, step_size, decay_rate * step_size, carried_state, skip_weight_per_head)
        return gate_norm(values, own_z, norm_gain, GROUPS)
    hidden = lax.map(one_request, (suffix_x.reshape(REQUESTS, SPAN, HEADS, P_SIZE), suffix_z.reshape(REQUESTS, SPAN, HEADS * P_SIZE), suffix_b.reshape(REQUESTS, SPAN, GROUPS, N), suffix_c.reshape(REQUESTS, SPAN, GROUPS, N), suffix_dt.reshape(REQUESTS, SPAN, HEADS), missed_x.reshape(REQUESTS, MISS_MAX, SPAN, HEADS, P_SIZE), missed_b.reshape(REQUESTS, MISS_MAX, SPAN, GROUPS, N), missed_dt.reshape(REQUESTS, MISS_MAX, SPAN, HEADS), page_index, missed)).reshape(TOKENS, HEADS * P_SIZE)
    set_width = HEADS // N_TENSOR * P_SIZE
    summed = jnp.zeros((TOKENS, D), jnp.float32)
    for set_index in range(N_TENSOR):
        lower = set_index * set_width
        partial_out = jnp.dot(hidden[:, lower:lower + set_width], out_weight[lower:lower + set_width], preferred_element_type=jnp.float32).astype(jnp.bfloat16)
        summed = summed + lax.optimization_barrier(partial_out).astype(jnp.float32)
    return summed.astype(jnp.bfloat16)
```

```python
import functools

import jax
import jax.numpy as jnp
from jax import lax
from jax.experimental import pallas as pl
from jax.experimental.pallas import tpu as pltpu
from jax.sharding import PartitionSpec as P

MESH = pl.DeviceIdType.MESH
P_SIZE = 64
N = 256
SPAN = 128
MISS = 3
REQ = 2
HEADS = 16
WIDTH = HEADS * P_SIZE
X = 4
ROWS = 32
F32 = jnp.float32
BF16 = jnp.bfloat16
NT = (((1,), (1,)), ((), ()))
HIGHEST = lax.Precision.HIGHEST


def dot(a, b, precision=None):
    return jnp.dot(a, b, preferred_element_type=F32, precision=precision)


def dot_nt(a, b):
    return lax.dot_general(a, b, NT, preferred_element_type=F32)


def iota(shape, dim):
    return lax.broadcasted_iota(jnp.int32, shape, dim)


def split(v):
    high = v.astype(BF16)
    return jnp.concatenate([high, (v - high.astype(F32)).astype(BF16)], axis=1)


def kernel(
    Z, T,
    picks, reqs, places, missed, dt_ref, bias, a_log, skip, gain,
    sx, sz, sb, sc, mx, mb, w_ref, cache,
    out_ref,
    wt, cg, outp, pg, relay, sp, rp, pt, a0, a1, xs, qs, hid,
    cs, cr, ws, wr, wxs, wxr, wfs, wfr, pgs, pgr, pjs, pjr,
    xsend, xrecv, ysend, yrecv, coresem_s, coresem_r, ys_s, ys_r,
):
    H = Z // 2
    r = lax.axis_index("replica")
    t = lax.axis_index("tensor")
    x = r // Z
    z = r % Z

    def zmod(v):
        return lax.rem(v + Z, Z)

    def at(xx, zz):
        return {"replica": lax.rem(xx + X, X) * Z + zmod(zz), "tensor": t}

    right_x, left_x = at(x + 1, z), at(x - 1, z)
    up_z, down_z = at(x, z + 1), at(x, z - 1)
    peers = [at(x, z + s) for s in range(1, Z)] + [right_x, left_x]
    if T > 1:
        y, c = t // 2, t % 2
        Y = T // 2
        other = {"replica": r, "tensor": y * 2 + 1 - c}
        y_up = {"replica": r, "tensor": lax.rem(y + 1, Y) * 2 + c}
        y_down = {"replica": r, "tensor": lax.rem(y + Y - 1, Y) * 2 + c}
        peers += [other, y_up, y_down]

    barrier = pltpu.get_barrier_semaphore()
    for peer in peers:
        pl.semaphore_signal(barrier, inc=1, device_id=peer, device_id_type=MESH)

    def w_rows(xx, zz, lo=0, count=64):
        start = (lax.rem(xx + X, X) * Z + zmod(zz)) * 64 + lo
        return wt.at[pl.ds(pl.multiple_of(start, 16), count)]

    eye64 = (iota((64, 64), 0) == iota((64, 64), 1)).astype(BF16)
    wt[pl.ds(pl.multiple_of(r * 64, 16), 64), :] = dot_nt(eye64, w_ref[...]).astype(BF16)
    cg[z] = sc[...]

    def fetch(k, carry):
        for g in range(4):
            for s in range(2):
                page = cache[picks[(g * Z + k) * 2 + s]]
                if g == 0:
                    pg[0, k, s * ROWS:(s + 1) * ROWS, :] = page
                else:
                    outp[g - 1, k, s * ROWS:(s + 1) * ROWS, :] = page
        return carry

    lax.fori_loop(0, Z, fetch, 0)
    pl.semaphore_wait(barrier, len(peers))

    sends = []

    def send(src, dst, ssem, rsem, device):
        copy = pltpu.make_async_remote_copy(
            src_ref=src, dst_ref=dst, send_sem=ssem, recv_sem=rsem,
            device_id=device, device_id_type=MESH,
        )
        copy.start()
        sends.append(copy)

    def arrived(ref, ssem, rsem, device):
        pltpu.make_async_remote_copy(
            src_ref=ref, dst_ref=ref, send_sem=ssem, recv_sem=rsem,
            device_id=device, device_id_type=MESH,
        ).wait_recv()

    def c_part(d, step):
        block = zmod(z - step) if d == 0 else zmod(z + step)
        if step < H:
            return cg.at[block]
        return cg.at[block, pl.ds(d * SPAN, SPAN)]

    def c_send(d, step):
        block = zmod(z - step + 1) if d == 0 else zmod(z + step - 1)
        part = cg.at[block] if step < H else cg.at[block, pl.ds(d * SPAN, SPAN)]
        send(part, part, cs.at[d, step - 1], cr.at[d, step - 1], (up_z, down_z)[d])

    def w_part(d, step):
        zz = z - step if d == 0 else z + step
        return w_rows(x, zz) if step < H else w_rows(x, zz, d * 32, 32)

    def w_send(d, step):
        zz = z - step + 1 if d == 0 else z + step - 1
        part = w_rows(x, zz) if step < H else w_rows(x, zz, d * 32, 32)
        send(part, part, ws.at[d, step - 1], wr.at[d, step - 1], (up_z, down_z)[d])

    def z_of(k):
        if k == 0:
            return z
        step = (k + 1) // 2
        return z - step if k % 2 == 1 else z + step

    def wx_send(k):
        part = w_rows(x, z_of(k))
        send(part, part, wxs.at[0, k], wxr.at[0, k], right_x)
        send(part, part, wxs.at[1, k], wxr.at[1, k], left_x)

    def wx_pass(k):
        arrived(w_rows(x - 1, z_of(k)), wxs.at[0, k], wxr.at[0, k], right_x)
        part = w_rows(x - 1, z_of(k), 0, 32)
        send(part, part, wfs.at[0, k], wfr.at[0, k], right_x)
        arrived(w_rows(x + 1, z_of(k)), wxs.at[1, k], wxr.at[1, k], left_x)
        part = w_rows(x + 1, z_of(k), 32, 32)
        send(part, part, wfs.at[1, k], wfr.at[1, k], left_x)

    send(outp.at[2, pl.ds(0, H)], relay.at[0], pgs.at[0], pgr.at[0], right_x)
    send(outp.at[2, pl.ds(H, H)], relay.at[1], pgs.at[1], pgr.at[1], left_x)
    c_send(0, 1)
    c_send(1, 1)
    send(outp.at[0], pg.at[1], pgs.at[2], pgr.at[2], right_x)
    send(outp.at[1], pg.at[2], pgs.at[3], pgr.at[3], left_x)
    w_send(0, 1)
    w_send(1, 1)

    def pages_pass():
        arrived(relay.at[0], pgs.at[0], pgr.at[0], right_x)
        send(relay.at[0], pg.at[3, pl.ds(0, H)], pgs.at[4], pgr.at[4], right_x)
        arrived(relay.at[1], pgs.at[1], pgr.at[1], left_x)
        send(relay.at[1], pg.at[3, pl.ds(H, H)], pgs.at[5], pgr.at[5], left_x)

    def pages_wait():
        arrived(pg.at[1], pgs.at[2], pgr.at[2], right_x)
        arrived(pg.at[2], pgs.at[3], pgr.at[3], left_x)
        arrived(pg.at[3, pl.ds(0, H)], pgs.at[4], pgr.at[4], right_x)
        arrived(pg.at[3, pl.ds(H, H)], pgs.at[5], pgr.at[5], left_x)

    def project(dz):
        pages = jnp.concatenate([pg[g, dz] for g in range(4)], axis=0)
        full = dot_nt(pages, cg[dz])
        parts = []
        for k in range(8):
            second = reqs[dz * 8 + k]
            rows = full[k * ROWS:(k + 1) * ROWS]
            parts.append(rows[:, :SPAN] * (1.0 - second) + rows[:, SPAN:] * second)
        return jnp.stack(parts).astype(BF16)

    def rp_of(zz):
        return rp.at[pl.ds(zz * 2 * X, 2 * X)]

    def project_send(dz, sem):
        sp[sem] = project(dz)
        send(sp.at[sem], rp_of(z), pjs.at[sem], pjr.at[sem], at(x, dz))

    def project_step(step):
        if step == 0:
            rp[pl.ds(z * 2 * X, 2 * X)] = project(z)
            return
        project_send(zmod(z + step), 2 * step - 2)
        if step < H:
            project_send(zmod(z - step), 2 * step - 1)

    lane = iota((1, SPAN), 1)
    lane_block = (lane // HEADS) % 4

    def decays():
        rows, cols = iota((SPAN, SPAN), 0), iota((SPAN, SPAN), 1)
        first = lane < 64
        count = jnp.where(first, missed[0], missed[1])
        active = jnp.where(lane_block == 3, 1, (lane_block >= MISS - count).astype(jnp.int32))
        active = active.astype(F32)
        raw = dt_ref[...] + bias[...]
        dt = jnp.maximum(raw, 0.0) + jnp.log1p(jnp.exp(-jnp.abs(raw)))
        dt = dt * active
        q = dot((rows >= cols).astype(F32), -jnp.exp(a_log[...]) * dt, HIGHEST)
        row_block, col_block = (rows // HEADS) % 4, (cols // HEADS) % 4
        later = (row_block < 3) & ((row_block >= col_block) | (col_block == 3))
        same = (rows // 64 == cols // 64) & (rows % HEADS == cols % HEADS)
        last = jnp.broadcast_to(q[SPAN - 1:, :], (8, SPAN))
        tail = dot(last, (later & same).astype(F32), HIGHEST)[0:1]
        weight = jnp.exp(jnp.where(lane_block == 3, q, tail - q))
        weight = jnp.where(lane_block == 3, weight, weight * dt)
        qs[0] = q
        qs[1] = q.T
        qs[2] = dt.T
        qs[3] = weight
        qs[4] = jnp.exp(jnp.where(lane_block == 3, q + tail, 0.0))

    def spread(values, block):
        chosen = jnp.where(lane // HEADS == block, values, 0.0)
        heads = iota((2 * SPAN, WIDTH), 0) % HEADS
        picked = (heads == iota((2 * SPAN, WIDTH), 1) // P_SIZE).astype(BF16)
        return dot(split(chosen), picked)

    def missed_block(q_, b):
        weight = spread(qs[3], q_ * 4 + b)
        at_ = (q_ * MISS + b) * SPAN
        xs[b * SPAN:(b + 1) * SPAN, :] = (mx[at_:at_ + SPAN, :].astype(F32) * weight).astype(BF16)

    def carried(q_):
        rows = slice(q_ * SPAN, (q_ + 1) * SPAN)
        scores = dot_nt(sc[rows, :], mb[q_ * MISS * SPAN:(q_ + 1) * MISS * SPAN, :])
        rest = dot(scores.astype(BF16), xs[...])
        a0[rows, :] = rest * spread(qs[3], q_ * 4 + 3) + skip[...] * sx[rows, :].astype(F32)
        qs[5] = dot_nt(sc[rows, :], sb[rows, :])

    def pair(q_, p):
        rows = slice(q_ * SPAN, (q_ + 1) * SPAN)
        cols = slice(p * 2 * P_SIZE, (p + 1) * 2 * P_SIZE)
        causal = iota((SPAN, SPAN), 0) >= iota((SPAN, SPAN), 1)
        mixes = []
        for h in range(2):
            at_ = q_ * 64 + 48 + p * 2 + h
            gap = jnp.where(causal, qs[0, :, at_:at_ + 1] - qs[1, at_:at_ + 1, :], -jnp.inf)
            mixes.append((jnp.exp(gap) * qs[2, at_:at_ + 1, :] * qs[5]).astype(BF16))
        two = sx[rows, cols]
        low = iota((SPAN, 2 * P_SIZE), 1) < P_SIZE
        zero = jnp.zeros_like(two)
        stacked = jnp.concatenate([jnp.where(low, two, zero), jnp.where(low, zero, two)], axis=0)
        a0[rows, cols] += dot(jnp.concatenate(mixes, axis=1), stacked)

    def gates(q_):
        rows = slice(q_ * SPAN, (q_ + 1) * SPAN)
        v = sz[rows, :].astype(F32)
        gate = v / (1.0 + jnp.exp(-v))
        a0[rows, :] = a0[rows, :] * gate
        a1[rows, :] = spread(qs[4], q_ * 4 + 3) * gate

    work = [decays]
    for q_ in range(REQ):
        work += [functools.partial(missed_block, q_, b) for b in range(MISS)]
        work.append(functools.partial(carried, q_))
        work += [functools.partial(pair, q_, p) for p in range(HEADS // 2)]
        work.append(functools.partial(gates, q_))

    LAG = min(3, H)
    steps = H + LAG + 1
    share = -(-len(work) // steps)
    wx_send(0)
    for i in range(1, steps + 1):
        if i <= H:
            for d in range(2):
                arrived(c_part(d, i), cs.at[d, i - 1], cr.at[d, i - 1], (up_z, down_z)[d])
                if i < H:
                    c_send(d, i + 1)
            for d in range(2):
                arrived(w_part(d, i), ws.at[d, i - 1], wr.at[d, i - 1], (up_z, down_z)[d])
                if i < H:
                    w_send(d, i + 1)
            if i < H:
                wx_send(2 * i - 1)
                wx_send(2 * i)
            else:
                wx_send(2 * H - 1)
        if i == 2 or H == 1:
            pages_pass()
        if i == LAG + 1:
            pages_wait()
        if i > LAG:
            if i == LAG + 1:
                project_step(0)
            if i - LAG <= H:
                project_step(i - LAG)
        for _ in range(share):
            if work:
                work.pop(0)()
        if i == 2:
            wx_pass(0)
        if 3 <= i <= H + 2:
            for k in (2 * (i - 2) - 1, 2 * (i - 2)):
                if k < Z:
                    wx_pass(k)
    while work:
        work.pop(0)()

    for step in range(1, H + 1):
        arrived(rp_of(zmod(z - step)), pjs.at[2 * step - 2], pjr.at[2 * step - 2], up_z)
        if step < H:
            arrived(rp_of(zmod(z + step)), pjs.at[2 * step - 1], pjr.at[2 * step - 1], up_z)

    eye = (iota((SPAN, SPAN), 0) == iota((SPAN, SPAN), 1)).astype(BF16)
    for q_ in range(REQ):
        def place(j, carry, q_=q_):
            pt[j] = rp[places[q_ * 2 * HEADS + j]]
            return carry

        lax.fori_loop(0, 2 * HEADS, place, 0, unroll=8)
        rows = slice(q_ * SPAN, (q_ + 1) * SPAN)
        g = a0[rows, :] + a1[rows, :] * dot_nt(eye, pt[...].reshape(WIDTH, SPAN))
        scale = lax.rsqrt(jnp.mean(g * g, axis=-1, keepdims=True) + 1e-05)
        hid[rows, :] = (g * scale * gain[...]).astype(BF16)

    for k in range(Z):
        arrived(w_rows(x + 2, z_of(k), 0, 32), wfs.at[0, k], wfr.at[0, k], right_x)
        arrived(w_rows(x + 2, z_of(k), 32, 32), wfs.at[1, k], wfr.at[1, k], left_x)

    cols = out_ref.shape[1]

    def product(block):
        weights = wt[pl.ds(pl.multiple_of(block * cols, cols), cols), :]
        return dot_nt(hid[...], weights)

    if T == 1:
        out_ref[...] = product(0).astype(BF16)
    else:
        offsets = (2, 1, Y - 1, 0)

        def block_of(k, core):
            return lax.rem(y + offsets[k], Y) * 2 + core

        for k in range(4):
            xsend[k] = product(block_of(k, 1 - c)).astype(BF16)
            send(xsend.at[k], xrecv.at[k], coresem_s.at[k], coresem_r.at[k], other)

        def both(k):
            mine = product(block_of(k, c))
            arrived(xrecv.at[k], coresem_s.at[k], coresem_r.at[k], other)
            return mine + xrecv[k].astype(F32)

        half = out_ref.shape[0] // 2
        lo, hi = pl.ds(0, half), pl.ds(half, half)
        ysend[0] = both(0).astype(BF16)
        send(ysend.at[0, lo], yrecv.at[0], ys_s.at[0], ys_r.at[0], y_up)
        send(ysend.at[0, hi], yrecv.at[1], ys_s.at[1], ys_r.at[1], y_down)
        up = both(1)
        ysend[1, hi] = up[half:].astype(BF16)
        send(ysend.at[1, hi], yrecv.at[2], ys_s.at[2], ys_r.at[2], y_up)
        down = both(2)
        ysend[2, lo] = down[:half].astype(BF16)
        send(ysend.at[2, lo], yrecv.at[3], ys_s.at[3], ys_r.at[3], y_down)
        arrived(yrecv.at[0], ys_s.at[0], ys_r.at[0], y_up)
        ysend[1, lo] = (up[:half] + yrecv[0].astype(F32)).astype(BF16)
        send(ysend.at[1, lo], yrecv.at[4], ys_s.at[4], ys_r.at[4], y_up)
        arrived(yrecv.at[1], ys_s.at[1], ys_r.at[1], y_down)
        ysend[2, hi] = (down[half:] + yrecv[1].astype(F32)).astype(BF16)
        send(ysend.at[2, hi], yrecv.at[5], ys_s.at[5], ys_r.at[5], y_down)
        own = both(3)
        for k in range(2, 6):
            arrived(yrecv.at[k], ys_s.at[k], ys_r.at[k], (y_up, y_down)[k % 2])
        low = own[:half] + yrecv[4].astype(F32) + yrecv[3].astype(F32)
        high = own[half:] + yrecv[2].astype(F32) + yrecv[5].astype(F32)
        out_ref[lo, :] = low.astype(BF16)
        out_ref[hi, :] = high.astype(BF16)

    for copy in sends:
        copy.wait_send()


def per_device(
    suffix_x, suffix_z, suffix_b, suffix_c, suffix_dt, missed_x, missed_b, missed_dt,
    dt_bias, a_log, skip_weight_per_head, norm_gain, out_weight, cache_pages,
    hit_holder, hit_slot, missed,
):
    R = lax.axis_size("replica")
    T = lax.axis_size("tensor")
    Z = R // X
    H = Z // 2
    r = lax.axis_index("replica")
    x, z = r // Z, r % Z
    hits = hit_holder.shape[1] * hit_holder.shape[2] // R
    holders = hit_holder[0, :, :, 0].reshape(R, hits)
    slots = hit_slot[0].reshape(R, hits)
    keys = jnp.arange(hits, dtype=jnp.int32) * 64 + slots

    def ends(mask, values):
        first = jnp.min(jnp.where(mask, values, 1 << 20), axis=-1)
        last = jnp.max(jnp.where(mask, values, -1), axis=-1)
        none = last < 0
        return jnp.stack([jnp.where(none, 0, first), jnp.where(none, 0, last)], axis=-1)

    out_order = (x + jnp.array([0, 1, 3, 2])) % X
    picks = (ends(holders == r, keys) % 64).reshape(X, Z, 2)[out_order].reshape(-1)
    in_order = (x + jnp.array([0, 3, 1, 2])) % X
    column = lax.dynamic_slice_in_dim(holders, x * Z, Z)
    column_keys = lax.dynamic_slice_in_dim(keys, x * Z, Z)
    wanted = column[None] == (in_order * Z + z)[:, None, None]
    reqs = ends(wanted, jnp.broadcast_to(column_keys[None], wanted.shape)) // (64 * hits // REQ)
    reqs = reqs.transpose(1, 0, 2).reshape(-1).astype(F32)
    own = lax.dynamic_index_in_dim(holders, r, 0, keepdims=False)
    positions = jnp.arange(hits)
    again = jnp.any((own[None] == own[:, None]) & (positions[None] < positions[:, None]), axis=1)
    relative = (x - own // Z + X) % X
    group = jnp.where(relative >= 2, 5 - relative, relative)
    places = (own % Z) * 8 + group * 2 + again.astype(jnp.int32)

    raw = jnp.concatenate(
        [missed_dt.reshape(REQ, MISS, SPAN, HEADS), suffix_dt.reshape(REQ, 1, SPAN, HEADS)], axis=1
    ).transpose(2, 0, 1, 3).reshape(SPAN, REQ * (MISS + 1) * HEADS)
    bias = jnp.tile(dt_bias, REQ * (MISS + 1))[None]
    rates = jnp.tile(a_log, REQ * (MISS + 1))[None]
    skip = jnp.repeat(skip_weight_per_head, P_SIZE)[None]

    smem = pl.BlockSpec(memory_space=pltpu.SMEM)
    vmem = pl.BlockSpec(memory_space=pltpu.VMEM)
    tokens = REQ * SPAN
    cols = out_weight.shape[1] * R // T
    V = pltpu.VMEM
    D = pltpu.SemaphoreType.DMA
    return pl.pallas_call(
        functools.partial(kernel, Z, T),
        out_shape=jax.ShapeDtypeStruct((tokens, cols), BF16),
        in_specs=[smem] * 4 + [vmem] * 13,
        out_specs=vmem,
        scratch_shapes=[
            V((R * 64, WIDTH), BF16),
            V((Z, tokens, N), BF16),
            V((3, Z, 2 * ROWS, N), BF16),
            V((4, Z, 2 * ROWS, N), BF16),
            V((2, H, 2 * ROWS, N), BF16),
            V((Z - 1, 2 * X, ROWS, SPAN), BF16),
            V((Z * 2 * X, ROWS, SPAN), BF16),
            V((2 * HEADS, ROWS, SPAN), BF16),
            V((tokens, WIDTH), F32),
            V((tokens, WIDTH), F32),
            V((MISS * SPAN, WIDTH), BF16),
            V((6, SPAN, SPAN), F32),
            V((tokens, WIDTH), BF16),
            D((2, H)), D((2, H)), D((2, H)), D((2, H)),
            D((2, Z)), D((2, Z)), D((2, Z)), D((2, Z)),
            D((6,)), D((6,)), D((Z - 1,)), D((Z - 1,)),
            V((4, tokens, cols), BF16),
            V((4, tokens, cols), BF16),
            V((3, tokens, cols), BF16),
            V((6, tokens // 2, cols), BF16),
            D((4,)), D((4,)), D((6,)), D((6,)),
        ],
        compiler_params=pltpu.CompilerParams(
            collective_id=0, has_side_effects=True, vmem_limit_bytes=58 * 1024 * 1024
        ),
        cost_estimate=pl.CostEstimate(
            flops=4 * 10**9, bytes_accessed=8 * 10**6, transcendentals=10**6
        ),
    )(
        picks.astype(jnp.int32), reqs, places.astype(jnp.int32), missed,
        raw, bias, rates, skip, norm_gain[None],
        suffix_x, suffix_z, suffix_b, suffix_c, missed_x, missed_b, out_weight,
        cache_pages[:, 0],
    )


def solution(mesh):
    in_specs = (
        P("replica", "tensor"),
        P("replica", "tensor"),
        P("replica", "tensor"),
        P("replica", "tensor"),
        P("replica", "tensor"),
        P("replica", "tensor"),
        P("replica", "tensor"),
        P("replica", "tensor"),
        P("tensor"),
        P("tensor"),
        P("tensor"),
        P("tensor"),
        P("tensor", "replica"),
        P("replica", "tensor", None, None),
        P("tensor", None, None, None),
        P("tensor", None, None),
        P("replica"),
    )
    return jax.shard_map(
        per_device, mesh=mesh, in_specs=in_specs, out_specs=P("replica", "tensor"), check_vma=False
    )
```

```python
import functools

import jax
import jax.numpy as jnp
from jax import lax
from jax.experimental import pallas as pl
from jax.experimental.pallas import tpu as pltpu
from jax.sharding import PartitionSpec as P

MESH = pl.DeviceIdType.MESH
P_SIZE = 64
N = 256
SPAN = 128
MISS = 3
REQ = 2
HEADS = 16
WIDTH = HEADS * P_SIZE
X = 4
ROWS = 32
PAGES = 32
F32 = jnp.float32
BF16 = jnp.bfloat16
NT = (((1,), (1,)), ((), ()))
HIGHEST = lax.Precision.HIGHEST


def dot(a, b, precision=None):
    return jnp.dot(a, b, preferred_element_type=F32, precision=precision)


def dot_nt(a, b):
    return lax.dot_general(a, b, NT, preferred_element_type=F32)


def iota(shape, dim):
    return lax.broadcasted_iota(jnp.int32, shape, dim)


def split(v):
    high = v.astype(BF16)
    return jnp.concatenate([high, (v - high.astype(F32)).astype(BF16)], axis=1)


def kernel(
    Z, T,
    missed, bias, a_log, skip, holders, slots, sdt, mdt, gain,
    sx, sz, sb, sc, mx, mb, w_ref, cache,
    out_ref,
    tables, places, tables_v, places_v, table_sems, wt, cg, outp, pg, relay, sp, rp, pt, a0, a1, xs, qs, skips, hid,
    cs, cr, ws, wr, wxs, wxr, wfs, wfr, pgs, pgr, pjs, pjr,
    xsend, xrecv, ysend, yrecv, coresem_s, coresem_r, ys_s, ys_r,
):
    H = Z // 2
    r = lax.axis_index("replica")
    t = lax.axis_index("tensor")
    x = r // Z
    z = r % Z

    def zmod(v):
        return lax.rem(v + Z, Z)

    def at(xx, zz):
        return {"replica": lax.rem(xx + X, X) * Z + zmod(zz), "tensor": t}

    right_x, left_x = at(x + 1, z), at(x - 1, z)
    up_z, down_z = at(x, z + 1), at(x, z - 1)
    peers = [at(x, z + s) for s in range(1, Z)] + [right_x, left_x]
    if T > 1:
        y, c = t // 2, t % 2
        Y = T // 2
        other = {"replica": r, "tensor": y * 2 + 1 - c}
        y_up = {"replica": r, "tensor": lax.rem(y + 1, Y) * 2 + c}
        y_down = {"replica": r, "tensor": lax.rem(y + Y - 1, Y) * 2 + c}
        peers += [other, y_up, y_down]

    barrier = pltpu.get_barrier_semaphore()
    for peer in peers:
        pl.semaphore_signal(barrier, inc=1, device_id=peer, device_id_type=MESH)

    def w_rows(xx, zz, lo=0, count=64):
        start = (lax.rem(xx + X, X) * Z + zmod(zz)) * 64 + lo
        return wt.at[pl.ds(pl.multiple_of(start, 16), count)]

    wt[pl.ds(pl.multiple_of(r * 64, 16), 64), :] = w_ref[...]
    cg[z] = sc[...]

    requests = holders.shape[2]
    hold = holders[...].reshape(PAGES, requests)
    page_row, request = iota((PAGES, requests), 0), iota((PAGES, requests), 1)
    keys = ((request % REQ) * PAGES + page_row) * 64 + slots[...]
    even = request[0:1] % REQ == 0

    def ends(holder):
        mask = hold == holder
        first = jnp.min(jnp.where(mask, keys, 1 << 20), axis=0, keepdims=True)
        last = jnp.max(jnp.where(mask, keys, -1), axis=0, keepdims=True)
        first = jnp.minimum(first, pltpu.roll(first, requests - 1, 1))
        last = jnp.maximum(last, pltpu.roll(last, requests - 1, 1))
        none = last < 0
        return [jnp.where(none | ~even, 0, first), jnp.where(none | ~even, 0, last)]

    table_rows = [key & 63 for key in ends(r)]
    for offset in (0, X - 1, 1, 2):
        holder = lax.rem(x + offset, X) * Z + z
        table_rows += [(key >= PAGES * 64).astype(jnp.int32) for key in ends(holder)]
    table_rows += [jnp.zeros((1, requests), jnp.int32)] * (16 - len(table_rows))
    for k, row in enumerate(table_rows):
        tables_v[k:k + 1, :] = row

    columns = [
        jnp.sum(jnp.where(request == r * REQ + e, hold, 0), axis=1, keepdims=True) for e in range(REQ)
    ]
    same = page_row == request
    as_rows = [
        jnp.sum(jnp.where(same, jnp.broadcast_to(v, same.shape), 0), axis=0, keepdims=True)
        for v in columns
    ]
    inside, earlier = request < PAGES, request < page_row

    def seen(column, row, mask):
        return jnp.max(jnp.where((column == row) & mask, 1, 0), axis=1, keepdims=True)

    again = [
        seen(columns[0], as_rows[0], earlier),
        jnp.maximum(seen(columns[1], as_rows[0], inside), seen(columns[1], as_rows[1], earlier)),
    ]
    place_table = jnp.zeros((PAGES, requests), jnp.int32)
    for e in range(REQ):
        relative = lax.rem(x + X - columns[e] // Z, X)
        group = jnp.where(relative >= 2, 5 - relative, relative)
        value = (columns[e] % Z) * (2 * X) + group * 2 + again[e]
        place_table = jnp.where(request == e, jnp.broadcast_to(value, same.shape), place_table)
    places_v[...] = place_table
    to_scalars = [
        pltpu.make_async_copy(tables_v, tables, table_sems.at[0]),
        pltpu.make_async_copy(places_v, places, table_sems.at[1]),
    ]
    for copy in to_scalars:
        copy.start()

    def fetch(k, carry):
        for g, offset in enumerate((0, 1, X - 1, 2)):
            for s in range(2):
                page = cache[tables[s, (lax.rem(x + offset, X) * Z + k) * REQ], 0]
                if g == 0:
                    pg[0, k, s * ROWS:(s + 1) * ROWS, :] = page
                else:
                    outp[g - 1, k, s * ROWS:(s + 1) * ROWS, :] = page
        return carry


    sends = []

    def send(src, dst, ssem, rsem, device):
        copy = pltpu.make_async_remote_copy(
            src_ref=src, dst_ref=dst, send_sem=ssem, recv_sem=rsem,
            device_id=device, device_id_type=MESH,
        )
        copy.start()
        sends.append(copy)

    def arrived(ref, ssem, rsem, device):
        pltpu.make_async_remote_copy(
            src_ref=ref, dst_ref=ref, send_sem=ssem, recv_sem=rsem,
            device_id=device, device_id_type=MESH,
        ).wait_recv()

    def c_part(d, step):
        block = zmod(z - step) if d == 0 else zmod(z + step)
        if step < H:
            return cg.at[block]
        return cg.at[block, pl.ds(d * SPAN, SPAN)]

    def c_send(d, step):
        block = zmod(z - step + 1) if d == 0 else zmod(z + step - 1)
        part = cg.at[block] if step < H else cg.at[block, pl.ds(d * SPAN, SPAN)]
        send(part, part, cs.at[d, step - 1], cr.at[d, step - 1], (up_z, down_z)[d])

    def w_part(d, step):
        zz = z - step if d == 0 else z + step
        return w_rows(x, zz) if step < H else w_rows(x, zz, d * 32, 32)

    def w_send(d, step):
        zz = z - step + 1 if d == 0 else z + step - 1
        part = w_rows(x, zz) if step < H else w_rows(x, zz, d * 32, 32)
        send(part, part, ws.at[d, step - 1], wr.at[d, step - 1], (up_z, down_z)[d])

    def z_of(k):
        if k == 0:
            return z
        step = (k + 1) // 2
        return z - step if k % 2 == 1 else z + step

    def wx_send(k):
        part = w_rows(x, z_of(k))
        send(part, part, wxs.at[0, k], wxr.at[0, k], right_x)
        send(part, part, wxs.at[1, k], wxr.at[1, k], left_x)

    def wx_pass(k):
        arrived(w_rows(x - 1, z_of(k)), wxs.at[0, k], wxr.at[0, k], right_x)
        part = w_rows(x - 1, z_of(k), 0, 32)
        send(part, part, wfs.at[0, k], wfr.at[0, k], right_x)
        arrived(w_rows(x + 1, z_of(k)), wxs.at[1, k], wxr.at[1, k], left_x)
        part = w_rows(x + 1, z_of(k), 32, 32)
        send(part, part, wfs.at[1, k], wfr.at[1, k], left_x)

    pl.semaphore_wait(barrier, len(peers))
    c_send(0, 1)
    c_send(1, 1)
    for copy in to_scalars:
        copy.wait()
    lax.fori_loop(0, Z, fetch, 0)
    send(outp.at[2, pl.ds(0, H)], relay.at[0], pgs.at[0], pgr.at[0], right_x)
    send(outp.at[2, pl.ds(H, H)], relay.at[1], pgs.at[1], pgr.at[1], left_x)
    send(outp.at[0], pg.at[1], pgs.at[2], pgr.at[2], right_x)
    send(outp.at[1], pg.at[2], pgs.at[3], pgr.at[3], left_x)
    w_send(0, 1)
    w_send(1, 1)

    def pages_pass():
        arrived(relay.at[0], pgs.at[0], pgr.at[0], right_x)
        send(relay.at[0], pg.at[3, pl.ds(0, H)], pgs.at[4], pgr.at[4], right_x)
        arrived(relay.at[1], pgs.at[1], pgr.at[1], left_x)
        send(relay.at[1], pg.at[3, pl.ds(H, H)], pgs.at[5], pgr.at[5], left_x)

    def pages_wait():
        arrived(pg.at[1], pgs.at[2], pgr.at[2], right_x)
        arrived(pg.at[2], pgs.at[3], pgr.at[3], left_x)
        arrived(pg.at[3, pl.ds(0, H)], pgs.at[4], pgr.at[4], right_x)
        arrived(pg.at[3, pl.ds(H, H)], pgs.at[5], pgr.at[5], left_x)

    def project(dz):
        pages = jnp.concatenate([pg[g, dz] for g in range(4)], axis=0)
        full = dot_nt(pages, cg[dz])
        parts = []
        for k in range(8):
            second = tables[2 + k, (x * Z + dz) * REQ].astype(F32)
            rows = full[k * ROWS:(k + 1) * ROWS]
            parts.append(rows[:, :SPAN] * (1.0 - second) + rows[:, SPAN:] * second)
        return jnp.stack(parts).astype(BF16)

    def rp_of(zz):
        return rp.at[pl.ds(zz * 2 * X, 2 * X)]

    def project_send(dz, sem):
        sp[sem] = project(dz)
        send(sp.at[sem], rp_of(z), pjs.at[sem], pjr.at[sem], at(x, dz))

    def project_step(step):
        if step == 0:
            rp[pl.ds(z * 2 * X, 2 * X)] = project(z)
            return
        project_send(zmod(z + step), 2 * step - 2)
        if step < H:
            project_send(zmod(z - step), 2 * step - 1)

    lane = iota((1, SPAN), 1)
    lane_block = (lane // HEADS) % 4

    def per_head(scalars):
        row = jnp.zeros((1, SPAN), F32)
        for h in range(HEADS):
            row = jnp.where(lane % HEADS == h, scalars[h], row)
        return row

    def decays():
        rows, cols = iota((SPAN, SPAN), 0), iota((SPAN, SPAN), 1)
        first = lane < 64
        count = jnp.where(first, missed[0], missed[1])
        active = jnp.where(lane_block == 3, 1, (lane_block >= MISS - count).astype(jnp.int32))
        active = active.astype(F32)
        steps = []
        for q_ in range(REQ):
            steps += [mdt[:, (q_ * MISS + b) * SPAN:(q_ * MISS + b + 1) * SPAN] for b in range(MISS)]
            steps.append(sdt[:, q_ * SPAN:(q_ + 1) * SPAN])
        raw = jnp.concatenate(steps, axis=0).T + per_head(bias)
        dt = jnp.maximum(raw, 0.0) + jnp.log1p(jnp.exp(-jnp.abs(raw)))
        dt = dt * active
        q = dot((rows >= cols).astype(F32), -jnp.exp(per_head(a_log)) * dt, HIGHEST)
        row_block, col_block = (rows // HEADS) % 4, (cols // HEADS) % 4
        later = (row_block < 3) & ((row_block >= col_block) | (col_block == 3))
        same = (rows // 64 == cols // 64) & (rows % HEADS == cols % HEADS)
        last = jnp.broadcast_to(q[SPAN - 1:, :], (8, SPAN))
        tail = dot(last, (later & same).astype(F32), HIGHEST)[0:1]
        weight = jnp.exp(jnp.where(lane_block == 3, q, tail - q))
        weight = jnp.where(lane_block == 3, weight, weight * dt)
        qs[0] = q
        qs[1] = q.T
        qs[2] = dt.T
        qs[3] = weight
        qs[4] = jnp.exp(jnp.where(lane_block == 3, q + tail, 0.0))
        skips[...] = spread(jnp.broadcast_to(per_head(skip), (8, SPAN)), 0)

    def spread(values, block):
        chosen = jnp.where(lane // HEADS == block, values, 0.0)
        heads = iota((2 * SPAN, WIDTH), 0) % HEADS
        picked = (heads == iota((2 * SPAN, WIDTH), 1) // P_SIZE).astype(BF16)
        return dot(split(chosen), picked)

    def missed_block(q_, b):
        weight = spread(qs[3], q_ * 4 + b)
        at_ = (q_ * MISS + b) * SPAN
        xs[b * SPAN:(b + 1) * SPAN, :] = (mx[at_:at_ + SPAN, :].astype(F32) * weight).astype(BF16)

    def carried(q_):
        rows = slice(q_ * SPAN, (q_ + 1) * SPAN)
        scores = dot_nt(sc[rows, :], mb[q_ * MISS * SPAN:(q_ + 1) * MISS * SPAN, :])
        rest = dot(scores.astype(BF16), xs[...])
        a0[rows, :] = rest * spread(qs[3], q_ * 4 + 3) + skips[0:1, :] * sx[rows, :].astype(F32)
        qs[5] = dot_nt(sc[rows, :], sb[rows, :])

    def pair(q_, p):
        rows = slice(q_ * SPAN, (q_ + 1) * SPAN)
        cols = slice(p * 2 * P_SIZE, (p + 1) * 2 * P_SIZE)
        causal = iota((SPAN, SPAN), 0) >= iota((SPAN, SPAN), 1)
        mixes = []
        for h in range(2):
            at_ = q_ * 64 + 48 + p * 2 + h
            gap = jnp.where(causal, qs[0, :, at_:at_ + 1] - qs[1, at_:at_ + 1, :], -jnp.inf)
            mixes.append((jnp.exp(gap) * qs[2, at_:at_ + 1, :] * qs[5]).astype(BF16))
        two = sx[rows, cols]
        low = iota((SPAN, 2 * P_SIZE), 1) < P_SIZE
        zero = jnp.zeros_like(two)
        stacked = jnp.concatenate([jnp.where(low, two, zero), jnp.where(low, zero, two)], axis=0)
        a0[rows, cols] += dot(jnp.concatenate(mixes, axis=1), stacked)

    def gates(q_):
        rows = slice(q_ * SPAN, (q_ + 1) * SPAN)
        v = sz[rows, :].astype(F32)
        gate = v / (1.0 + jnp.exp(-v))
        a0[rows, :] = a0[rows, :] * gate
        a1[rows, :] = spread(qs[4], q_ * 4 + 3) * gate

    work = [decays]
    for q_ in range(REQ):
        work += [functools.partial(missed_block, q_, b) for b in range(MISS)]
        work.append(functools.partial(carried, q_))
        work += [functools.partial(pair, q_, p) for p in range(HEADS // 2)]
        work.append(functools.partial(gates, q_))

    LAG = min(3, H)
    steps = H + LAG + 1
    share = -(-len(work) // steps)
    wx_send(0)
    for i in range(1, steps + 1):
        if i <= H:
            for d in range(2):
                arrived(c_part(d, i), cs.at[d, i - 1], cr.at[d, i - 1], (up_z, down_z)[d])
                if i < H:
                    c_send(d, i + 1)
            for d in range(2):
                arrived(w_part(d, i), ws.at[d, i - 1], wr.at[d, i - 1], (up_z, down_z)[d])
                if i < H:
                    w_send(d, i + 1)
            if i < H:
                wx_send(2 * i - 1)
                wx_send(2 * i)
            else:
                wx_send(2 * H - 1)
        if i == 2 or H == 1:
            pages_pass()
        if i == LAG + 1:
            pages_wait()
        if i > LAG:
            if i == LAG + 1:
                project_step(0)
            if i - LAG <= H:
                project_step(i - LAG)
        for _ in range(share):
            if work:
                work.pop(0)()
        if i == 2:
            wx_pass(0)
        if 3 <= i <= H + 2:
            for k in (2 * (i - 2) - 1, 2 * (i - 2)):
                if k < Z:
                    wx_pass(k)
    while work:
        work.pop(0)()

    for step in range(1, H + 1):
        arrived(rp_of(zmod(z - step)), pjs.at[2 * step - 2], pjr.at[2 * step - 2], up_z)
        if step < H:
            arrived(rp_of(zmod(z + step)), pjs.at[2 * step - 1], pjr.at[2 * step - 1], up_z)

    eye = (iota((SPAN, SPAN), 0) == iota((SPAN, SPAN), 1)).astype(BF16)
    for q_ in range(REQ):
        def place(j, carry, q_=q_):
            pt[j] = rp[places[j, q_]]
            return carry

        lax.fori_loop(0, 2 * HEADS, place, 0, unroll=8)
        rows = slice(q_ * SPAN, (q_ + 1) * SPAN)
        g = a0[rows, :] + a1[rows, :] * dot_nt(eye, pt[...].reshape(WIDTH, SPAN))
        scale = lax.rsqrt(jnp.mean(g * g, axis=-1, keepdims=True) + 1e-05)
        hid[rows, :] = (g * scale * gain[...]).astype(BF16)

    for k in range(Z):
        arrived(w_rows(x + 2, z_of(k), 0, 32), wfs.at[0, k], wfr.at[0, k], right_x)
        arrived(w_rows(x + 2, z_of(k), 32, 32), wfs.at[1, k], wfr.at[1, k], left_x)

    cols = out_ref.shape[1]

    def product(block):
        weights = wt[pl.ds(pl.multiple_of(block * cols, cols), cols), :]
        return dot_nt(hid[...], weights)

    if T == 1:
        out_ref[...] = product(0).astype(BF16)
    else:
        offsets = (2, 1, Y - 1, 0)

        def block_of(k, core):
            return lax.rem(y + offsets[k], Y) * 2 + core

        for k in range(4):
            xsend[k] = product(block_of(k, 1 - c)).astype(BF16)
            send(xsend.at[k], xrecv.at[k], coresem_s.at[k], coresem_r.at[k], other)

        def both(k):
            mine = product(block_of(k, c))
            arrived(xrecv.at[k], coresem_s.at[k], coresem_r.at[k], other)
            return mine + xrecv[k].astype(F32)

        half = out_ref.shape[0] // 2
        lo, hi = pl.ds(0, half), pl.ds(half, half)
        ysend[0] = both(0).astype(BF16)
        send(ysend.at[0, lo], yrecv.at[0], ys_s.at[0], ys_r.at[0], y_up)
        send(ysend.at[0, hi], yrecv.at[1], ys_s.at[1], ys_r.at[1], y_down)
        up = both(1)
        ysend[1, hi] = up[half:].astype(BF16)
        send(ysend.at[1, hi], yrecv.at[2], ys_s.at[2], ys_r.at[2], y_up)
        down = both(2)
        ysend[2, lo] = down[:half].astype(BF16)
        send(ysend.at[2, lo], yrecv.at[3], ys_s.at[3], ys_r.at[3], y_down)
        arrived(yrecv.at[0], ys_s.at[0], ys_r.at[0], y_up)
        ysend[1, lo] = (up[:half] + yrecv[0].astype(F32)).astype(BF16)
        send(ysend.at[1, lo], yrecv.at[4], ys_s.at[4], ys_r.at[4], y_up)
        arrived(yrecv.at[1], ys_s.at[1], ys_r.at[1], y_down)
        ysend[2, hi] = (down[half:] + yrecv[1].astype(F32)).astype(BF16)
        send(ysend.at[2, hi], yrecv.at[5], ys_s.at[5], ys_r.at[5], y_down)
        own = both(3)
        for k in range(2, 6):
            arrived(yrecv.at[k], ys_s.at[k], ys_r.at[k], (y_up, y_down)[k % 2])
        low = own[:half] + yrecv[4].astype(F32) + yrecv[3].astype(F32)
        high = own[half:] + yrecv[2].astype(F32) + yrecv[5].astype(F32)
        out_ref[lo, :] = low.astype(BF16)
        out_ref[hi, :] = high.astype(BF16)

    for copy in sends:
        copy.wait_send()


def per_device(
    suffix_x, suffix_z, suffix_b, suffix_c, suffix_dt, missed_x, missed_b, missed_dt,
    dt_bias, a_log, skip_weight_per_head, norm_gain, out_weight, cache_pages,
    hit_holder, hit_slot, missed,
):
    R = lax.axis_size("replica")
    T = lax.axis_size("tensor")
    Z = R // X
    H = Z // 2
    smem = pl.BlockSpec(memory_space=pltpu.SMEM)
    vmem = pl.BlockSpec(memory_space=pltpu.VMEM)
    tokens = REQ * SPAN
    cols = out_weight.shape[1] * R // T
    V = pltpu.VMEM
    D = pltpu.SemaphoreType.DMA
    return pl.pallas_call(
        functools.partial(kernel, Z, T),
        out_shape=jax.ShapeDtypeStruct((tokens, cols), BF16),
        in_specs=[smem] * 4 + [vmem] * 13,
        out_specs=vmem,
        scratch_shapes=[
            pltpu.SMEM((16, 2 * R), jnp.int32),
            pltpu.SMEM((PAGES, 2 * R), jnp.int32),
            V((16, 2 * R), jnp.int32),
            V((PAGES, 2 * R), jnp.int32),
            D((2,)),
            V((R * 64, WIDTH), BF16),
            V((Z, tokens, N), BF16),
            V((3, Z, 2 * ROWS, N), BF16),
            V((4, Z, 2 * ROWS, N), BF16),
            V((2, H, 2 * ROWS, N), BF16),
            V((Z - 1, 2 * X, ROWS, SPAN), BF16),
            V((Z * 2 * X, ROWS, SPAN), BF16),
            V((2 * HEADS, ROWS, SPAN), BF16),
            V((tokens, WIDTH), F32),
            V((tokens, WIDTH), F32),
            V((MISS * SPAN, WIDTH), BF16),
            V((6, SPAN, SPAN), F32),
            V((8, WIDTH), F32),
            V((tokens, WIDTH), BF16),
            D((2, H)), D((2, H)), D((2, H)), D((2, H)),
            D((2, Z)), D((2, Z)), D((2, Z)), D((2, Z)),
            D((6,)), D((6,)), D((Z - 1,)), D((Z - 1,)),
            V((4, tokens, cols), BF16),
            V((4, tokens, cols), BF16),
            V((3, tokens, cols), BF16),
            V((6, tokens // 2, cols), BF16),
            D((4,)), D((4,)), D((6,)), D((6,)),
        ],
        compiler_params=pltpu.CompilerParams(
            collective_id=0, has_side_effects=True, vmem_limit_bytes=58 * 1024 * 1024
        ),
        cost_estimate=pl.CostEstimate(
            flops=4 * 10**9, bytes_accessed=8 * 10**6, transcendentals=10**6
        ),
    )(
        missed, dt_bias, a_log, skip_weight_per_head,
        hit_holder[0].transpose(1, 2, 0), hit_slot[0].T, suffix_dt.T, missed_dt.T, norm_gain[None],
        suffix_x, suffix_z, suffix_b, suffix_c, missed_x, missed_b, out_weight.T, cache_pages,
    )


def solution(mesh):
    in_specs = (
        P("replica", "tensor"),
        P("replica", "tensor"),
        P("replica", "tensor"),
        P("replica", "tensor"),
        P("replica", "tensor"),
        P("replica", "tensor"),
        P("replica", "tensor"),
        P("replica", "tensor"),
        P("tensor"),
        P("tensor"),
        P("tensor"),
        P("tensor"),
        P("tensor", "replica"),
        P("replica", "tensor", None, None),
        P("tensor", None, None, None),
        P("tensor", None, None),
        P("replica"),
    )
    return jax.shard_map(
        per_device, mesh=mesh, in_specs=in_specs, out_specs=P("replica", "tensor"), check_vma=False
    )
```

```python
import functools

import jax
import jax.numpy as jnp
from jax import lax
from jax.experimental import pallas as pl
from jax.experimental.pallas import tpu as pltpu
from jax.sharding import PartitionSpec as P

MESH = pl.DeviceIdType.MESH
P_SIZE = 64
N = 256
SPAN = 128
MISS = 3
REQ = 2
HEADS = 16
WIDTH = HEADS * P_SIZE
X = 4
NCH = 4
ROWS = 32
PAGES = 32
F32 = jnp.float32
BF16 = jnp.bfloat16
NT = (((1,), (1,)), ((), ()))
HIGHEST = lax.Precision.HIGHEST


def dot(a, b, precision=None):
    return jnp.dot(a, b, preferred_element_type=F32, precision=precision)


def dot_nt(a, b):
    return lax.dot_general(a, b, NT, preferred_element_type=F32)


def iota(shape, dim):
    return lax.broadcasted_iota(jnp.int32, shape, dim)


def split(v):
    high = v.astype(BF16)
    return jnp.concatenate([high, (v - high.astype(F32)).astype(BF16)], axis=1)


def kernel(
    Z, T,
    missed, bias, a_log, skip, holders, slots, sdt, mdt, gain,
    sx, sz, sb, sc, mx, mb, w_ref, cache,
    out_ref,
    tables, places, tables_v, places_v, table_sems, wt, cg, outp, pg, relay, sp, rp, pt, a0, a1, xs, qs, skips, hid,
    cs, cr, ws, wr, wxs, wxr, wfs, wfr, pgs, pgr, pjs, pjr,
    xsend, xrecv, ysend, yrecv, coresem_s, coresem_r, ys_s, ys_r,
):
    H = Z // 2
    r = lax.axis_index("replica")
    t = lax.axis_index("tensor")
    x = r // Z
    z = r % Z

    def zmod(v):
        return lax.rem(v + Z, Z)

    def at(xx, zz):
        return {"replica": lax.rem(xx + X, X) * Z + zmod(zz), "tensor": t}

    right_x, left_x = at(x + 1, z), at(x - 1, z)
    up_z, down_z = at(x, z + 1), at(x, z - 1)
    peers = [at(x, z + s) for s in range(1, Z)] + [right_x, left_x]
    if T > 1:
        y, c = t // 2, t % 2
        Y = T // 2
        other = {"replica": r, "tensor": y * 2 + 1 - c}
        y_up = {"replica": r, "tensor": lax.rem(y + 1, Y) * 2 + c}
        y_down = {"replica": r, "tensor": lax.rem(y + Y - 1, Y) * 2 + c}
        peers += [other, y_up, y_down]

    barrier = pltpu.get_barrier_semaphore()
    for peer in peers:
        pl.semaphore_signal(barrier, inc=1, device_id=peer, device_id_type=MESH)

    def w_rows(xx, zz, lo=0, count=64):
        start = (lax.rem(xx + X, X) * Z + zmod(zz)) * 64 + lo
        return wt.at[pl.ds(pl.multiple_of(start, 16), count)]

    wt[pl.ds(pl.multiple_of(r * 64, 16), 64), :] = w_ref[...]
    cg[z] = sc[...]

    requests = holders.shape[2]
    hold = holders[...].reshape(PAGES, requests)
    page_row, request = iota((PAGES, requests), 0), iota((PAGES, requests), 1)
    keys = ((request % REQ) * PAGES + page_row) * 64 + slots[...]
    even = request[0:1] % REQ == 0

    def ends(holder):
        mask = hold == holder
        first = jnp.min(jnp.where(mask, keys, 1 << 20), axis=0, keepdims=True)
        last = jnp.max(jnp.where(mask, keys, -1), axis=0, keepdims=True)
        first = jnp.minimum(first, pltpu.roll(first, requests - 1, 1))
        last = jnp.maximum(last, pltpu.roll(last, requests - 1, 1))
        none = last < 0
        return [jnp.where(none | ~even, 0, first), jnp.where(none | ~even, 0, last)]

    table_rows = [key & 63 for key in ends(r)]
    for offset in (0, X - 1, 1, 2):
        holder = lax.rem(x + offset, X) * Z + z
        table_rows += [(key >= PAGES * 64).astype(jnp.int32) for key in ends(holder)]
    table_rows += [jnp.zeros((1, requests), jnp.int32)] * (16 - len(table_rows))
    for k, row in enumerate(table_rows):
        tables_v[k:k + 1, :] = row

    columns = [
        jnp.sum(jnp.where(request == r * REQ + e, hold, 0), axis=1, keepdims=True) for e in range(REQ)
    ]
    same = page_row == request
    as_rows = [
        jnp.sum(jnp.where(same, jnp.broadcast_to(v, same.shape), 0), axis=0, keepdims=True)
        for v in columns
    ]
    inside, earlier = request < PAGES, request < page_row

    def seen(column, row, mask):
        return jnp.max(jnp.where((column == row) & mask, 1, 0), axis=1, keepdims=True)

    again = [
        seen(columns[0], as_rows[0], earlier),
        jnp.maximum(seen(columns[1], as_rows[0], inside), seen(columns[1], as_rows[1], earlier)),
    ]
    place_table = jnp.zeros((PAGES, requests), jnp.int32)
    for e in range(REQ):
        relative = lax.rem(x + X - columns[e] // Z, X)
        group = jnp.where(relative >= 2, 5 - relative, relative)
        value = (columns[e] % Z) * (2 * X) + group * 2 + again[e]
        place_table = jnp.where(request == e, jnp.broadcast_to(value, same.shape), place_table)
    places_v[...] = place_table
    to_scalars = [
        pltpu.make_async_copy(tables_v, tables, table_sems.at[0]),
        pltpu.make_async_copy(places_v, places, table_sems.at[1]),
    ]
    for copy in to_scalars:
        copy.start()

    def fetch(k, carry):
        zz = zmod(z + (1 - 2 * (k % 2)) * ((k + 1) // 2))
        for g, offset in enumerate((0, 1, X - 1, 2)):
            for s in range(2):
                page = cache[tables[s, (lax.rem(x + offset, X) * Z + zz) * REQ], 0]
                if g == 0:
                    pg[0, k, s * ROWS:(s + 1) * ROWS, :] = page
                else:
                    outp[g - 1, k, s * ROWS:(s + 1) * ROWS, :] = page
        return carry


    sends = []

    def send(src, dst, ssem, rsem, device):
        copy = pltpu.make_async_remote_copy(
            src_ref=src, dst_ref=dst, send_sem=ssem, recv_sem=rsem,
            device_id=device, device_id_type=MESH,
        )
        copy.start()
        sends.append(copy)

    def arrived(ref, ssem, rsem, device):
        pltpu.make_async_remote_copy(
            src_ref=ref, dst_ref=ref, send_sem=ssem, recv_sem=rsem,
            device_id=device, device_id_type=MESH,
        ).wait_recv()

    def c_part(d, step):
        block = zmod(z - step) if d == 0 else zmod(z + step)
        if step < H:
            return cg.at[block]
        return cg.at[block, pl.ds(d * SPAN, SPAN)]

    def c_send(d, step):
        block = zmod(z - step + 1) if d == 0 else zmod(z + step - 1)
        part = cg.at[block] if step < H else cg.at[block, pl.ds(d * SPAN, SPAN)]
        send(part, part, cs.at[d, step - 1], cr.at[d, step - 1], (up_z, down_z)[d])

    def w_part(d, step):
        zz = z - step if d == 0 else z + step
        return w_rows(x, zz) if step < H else w_rows(x, zz, d * 32, 32)

    def w_send(d, step):
        zz = z - step + 1 if d == 0 else z + step - 1
        part = w_rows(x, zz) if step < H else w_rows(x, zz, d * 32, 32)
        send(part, part, ws.at[d, step - 1], wr.at[d, step - 1], (up_z, down_z)[d])

    def z_of(k):
        if k == 0:
            return z
        step = (k + 1) // 2
        return z - step if k % 2 == 1 else z + step

    def wx_send(k):
        part = w_rows(x, z_of(k))
        send(part, part, wxs.at[0, k], wxr.at[0, k], right_x)
        send(part, part, wxs.at[1, k], wxr.at[1, k], left_x)

    def wx_pass(k):
        arrived(w_rows(x - 1, z_of(k)), wxs.at[0, k], wxr.at[0, k], right_x)
        part = w_rows(x - 1, z_of(k), 0, 32)
        send(part, part, wfs.at[0, k], wfr.at[0, k], right_x)
        arrived(w_rows(x + 1, z_of(k)), wxs.at[1, k], wxr.at[1, k], left_x)
        part = w_rows(x + 1, z_of(k), 32, 32)
        send(part, part, wfs.at[1, k], wfr.at[1, k], left_x)

    pl.semaphore_wait(barrier, len(peers))
    c_send(0, 1)
    c_send(1, 1)
    for copy in to_scalars:
        copy.wait()
    CHUNK = Z // NCH
    HALF = CHUNK // 2
    for chunk in range(NCH):
        lax.fori_loop(chunk * CHUNK, (chunk + 1) * CHUNK, fetch, 0)
        whole = pl.ds(chunk * CHUNK, CHUNK)
        first, second = pl.ds(chunk * CHUNK, HALF), pl.ds(chunk * CHUNK + HALF, HALF)
        via = pl.ds(chunk * HALF, HALF)
        ss, rs = [pgs.at[chunk, k] for k in range(6)], [pgr.at[chunk, k] for k in range(6)]
        send(outp.at[2, first], relay.at[0, via], ss[0], rs[0], right_x)
        send(outp.at[2, second], relay.at[1, via], ss[1], rs[1], left_x)
        send(outp.at[0, whole], pg.at[1, whole], ss[2], rs[2], right_x)
        send(outp.at[1, whole], pg.at[2, whole], ss[3], rs[3], left_x)
        if chunk == 0:
            w_send(0, 1)
            w_send(1, 1)

    def pages_pass(chunk):
        first, second = pl.ds(chunk * CHUNK, HALF), pl.ds(chunk * CHUNK + HALF, HALF)
        via = pl.ds(chunk * HALF, HALF)
        ss, rs = [pgs.at[chunk, k] for k in range(6)], [pgr.at[chunk, k] for k in range(6)]
        arrived(relay.at[0, via], ss[0], rs[0], right_x)
        send(relay.at[0, via], pg.at[3, first], ss[4], rs[4], right_x)
        arrived(relay.at[1, via], ss[1], rs[1], left_x)
        send(relay.at[1, via], pg.at[3, second], ss[5], rs[5], left_x)

    def pages_wait(chunk):
        whole = pl.ds(chunk * CHUNK, CHUNK)
        first, second = pl.ds(chunk * CHUNK, HALF), pl.ds(chunk * CHUNK + HALF, HALF)
        ss, rs = [pgs.at[chunk, k] for k in range(6)], [pgr.at[chunk, k] for k in range(6)]
        arrived(pg.at[1, whole], ss[2], rs[2], right_x)
        arrived(pg.at[2, whole], ss[3], rs[3], left_x)
        arrived(pg.at[3, first], ss[4], rs[4], right_x)
        arrived(pg.at[3, second], ss[5], rs[5], left_x)

    def rp_of(zz):
        return rp.at[pl.ds(zz * 2 * X, 2 * X)]

    waited = set()

    def project(k):
        if k // CHUNK not in waited:
            waited.add(k // CHUNK)
            pages_wait(k // CHUNK)
        dz = zmod(z_of(k))
        pages = jnp.concatenate([pg[g, k] for g in range(4)], axis=0)
        full = dot_nt(pages, cg[dz])
        parts = []
        for slot in range(8):
            second = tables[2 + slot, (x * Z + dz) * REQ].astype(F32)
            rows = full[slot * ROWS:(slot + 1) * ROWS]
            parts.append(rows[:, :SPAN] * (1.0 - second) + rows[:, SPAN:] * second)
        products = jnp.stack(parts).astype(BF16)
        if k == 0:
            rp[pl.ds(z * 2 * X, 2 * X)] = products
        else:
            sp[k - 1] = products
            send(sp.at[k - 1], rp_of(z), pjs.at[k - 1], pjr.at[k - 1], at(x, dz))

    lane = iota((1, SPAN), 1)
    lane_block = (lane // HEADS) % 4

    def per_head(scalars):
        row = jnp.zeros((1, SPAN), F32)
        for h in range(HEADS):
            row = jnp.where(lane % HEADS == h, scalars[h], row)
        return row

    def decays():
        rows, cols = iota((SPAN, SPAN), 0), iota((SPAN, SPAN), 1)
        first = lane < 64
        count = jnp.where(first, missed[0], missed[1])
        active = jnp.where(lane_block == 3, 1, (lane_block >= MISS - count).astype(jnp.int32))
        active = active.astype(F32)
        steps = []
        for q_ in range(REQ):
            steps += [mdt[:, (q_ * MISS + b) * SPAN:(q_ * MISS + b + 1) * SPAN] for b in range(MISS)]
            steps.append(sdt[:, q_ * SPAN:(q_ + 1) * SPAN])
        raw = jnp.concatenate(steps, axis=0).T + per_head(bias)
        dt = jnp.maximum(raw, 0.0) + jnp.log1p(jnp.exp(-jnp.abs(raw)))
        dt = dt * active
        q = dot((rows >= cols).astype(F32), -jnp.exp(per_head(a_log)) * dt, HIGHEST)
        row_block, col_block = (rows // HEADS) % 4, (cols // HEADS) % 4
        later = (row_block < 3) & ((row_block >= col_block) | (col_block == 3))
        same = (rows // 64 == cols // 64) & (rows % HEADS == cols % HEADS)
        last = jnp.broadcast_to(q[SPAN - 1:, :], (8, SPAN))
        tail = dot(last, (later & same).astype(F32), HIGHEST)[0:1]
        weight = jnp.exp(jnp.where(lane_block == 3, q, tail - q))
        weight = jnp.where(lane_block == 3, weight, weight * dt)
        qs[0] = q
        qs[1] = q.T
        qs[2] = dt.T
        qs[3] = weight
        qs[4] = jnp.exp(jnp.where(lane_block == 3, q + tail, 0.0))
        skips[...] = spread(jnp.broadcast_to(per_head(skip), (8, SPAN)), 0)

    def spread(values, block):
        chosen = jnp.where(lane // HEADS == block, values, 0.0)
        heads = iota((2 * SPAN, WIDTH), 0) % HEADS
        picked = (heads == iota((2 * SPAN, WIDTH), 1) // P_SIZE).astype(BF16)
        return dot(split(chosen), picked)

    def missed_block(q_, b):
        weight = spread(qs[3], q_ * 4 + b)
        at_ = (q_ * MISS + b) * SPAN
        xs[b * SPAN:(b + 1) * SPAN, :] = (mx[at_:at_ + SPAN, :].astype(F32) * weight).astype(BF16)

    def carried(q_):
        rows = slice(q_ * SPAN, (q_ + 1) * SPAN)
        scores = dot_nt(sc[rows, :], mb[q_ * MISS * SPAN:(q_ + 1) * MISS * SPAN, :])
        rest = dot(scores.astype(BF16), xs[...])
        a0[rows, :] = rest * spread(qs[3], q_ * 4 + 3) + skips[0:1, :] * sx[rows, :].astype(F32)
        qs[5] = dot_nt(sc[rows, :], sb[rows, :])

    def pair(q_, p):
        rows = slice(q_ * SPAN, (q_ + 1) * SPAN)
        cols = slice(p * 2 * P_SIZE, (p + 1) * 2 * P_SIZE)
        causal = iota((SPAN, SPAN), 0) >= iota((SPAN, SPAN), 1)
        mixes = []
        for h in range(2):
            at_ = q_ * 64 + 48 + p * 2 + h
            gap = jnp.where(causal, qs[0, :, at_:at_ + 1] - qs[1, at_:at_ + 1, :], -jnp.inf)
            mixes.append((jnp.exp(gap) * qs[2, at_:at_ + 1, :] * qs[5]).astype(BF16))
        two = sx[rows, cols]
        low = iota((SPAN, 2 * P_SIZE), 1) < P_SIZE
        zero = jnp.zeros_like(two)
        stacked = jnp.concatenate([jnp.where(low, two, zero), jnp.where(low, zero, two)], axis=0)
        a0[rows, cols] += dot(jnp.concatenate(mixes, axis=1), stacked)

    def gates(q_):
        rows = slice(q_ * SPAN, (q_ + 1) * SPAN)
        v = sz[rows, :].astype(F32)
        gate = v / (1.0 + jnp.exp(-v))
        a0[rows, :] = a0[rows, :] * gate
        a1[rows, :] = spread(qs[4], q_ * 4 + 3) * gate

    work = [decays]
    for q_ in range(REQ):
        work += [functools.partial(missed_block, q_, b) for b in range(MISS)]
        work.append(functools.partial(carried, q_))
        work += [functools.partial(pair, q_, p) for p in range(HEADS // 2)]
        work.append(functools.partial(gates, q_))

    share = -(-len(work) // (H + 1))
    moved = passed = 0
    for i in range(1, H + 2):
        if i <= H:
            for d in range(2):
                arrived(c_part(d, i), cs.at[d, i - 1], cr.at[d, i - 1], (up_z, down_z)[d])
                if i < H:
                    c_send(d, i + 1)
        if i <= NCH:
            pages_pass(i - 1)
        if i > 1:
            for k in (2 * i - 3, 2 * i - 2):
                if k < Z:
                    project(k)
        if i <= H:
            for d in range(2):
                arrived(w_part(d, i), ws.at[d, i - 1], wr.at[d, i - 1], (up_z, down_z)[d])
                if i < H:
                    w_send(d, i + 1)
        if i >= NCH:
            while moved < min(2 * i + 1, Z):
                wx_send(moved)
                moved += 1
        for _ in range(share):
            if work:
                work.pop(0)()
        if i >= NCH + 2:
            for _ in range(2):
                wx_pass(passed)
                passed += 1
    while passed < Z:
        wx_pass(passed)
        passed += 1
    project(0)
    for k in range(1, Z):
        arrived(rp_of(zmod(2 * z - z_of(k))), pjs.at[k - 1], pjr.at[k - 1], up_z)

    eye = (iota((SPAN, SPAN), 0) == iota((SPAN, SPAN), 1)).astype(BF16)
    for q_ in range(REQ):
        def place(j, carry, q_=q_):
            pt[j] = rp[places[j, q_]]
            return carry

        lax.fori_loop(0, 2 * HEADS, place, 0, unroll=8)
        rows = slice(q_ * SPAN, (q_ + 1) * SPAN)
        g = a0[rows, :] + a1[rows, :] * dot_nt(eye, pt[...].reshape(WIDTH, SPAN))
        scale = lax.rsqrt(jnp.mean(g * g, axis=-1, keepdims=True) + 1e-05)
        hid[rows, :] = (g * scale * gain[...]).astype(BF16)

    for k in range(Z):
        arrived(w_rows(x + 2, z_of(k), 0, 32), wfs.at[0, k], wfr.at[0, k], right_x)
        arrived(w_rows(x + 2, z_of(k), 32, 32), wfs.at[1, k], wfr.at[1, k], left_x)

    cols = out_ref.shape[1]

    def product(block):
        weights = wt[pl.ds(pl.multiple_of(block * cols, cols), cols), :]
        return dot_nt(hid[...], weights)

    if T == 1:
        out_ref[...] = product(0).astype(BF16)
    else:
        offsets = (2, 1, Y - 1, 0)

        def block_of(k, core):
            return lax.rem(y + offsets[k], Y) * 2 + core

        for k in range(4):
            xsend[k] = product(block_of(k, 1 - c)).astype(BF16)
            send(xsend.at[k], xrecv.at[k], coresem_s.at[k], coresem_r.at[k], other)

        def both(k):
            mine = product(block_of(k, c))
            arrived(xrecv.at[k], coresem_s.at[k], coresem_r.at[k], other)
            return mine + xrecv[k].astype(F32)

        half = out_ref.shape[0] // 2
        lo, hi = pl.ds(0, half), pl.ds(half, half)
        ysend[0] = both(0).astype(BF16)
        send(ysend.at[0, lo], yrecv.at[0], ys_s.at[0], ys_r.at[0], y_up)
        send(ysend.at[0, hi], yrecv.at[1], ys_s.at[1], ys_r.at[1], y_down)
        up = both(1)
        ysend[1, hi] = up[half:].astype(BF16)
        send(ysend.at[1, hi], yrecv.at[2], ys_s.at[2], ys_r.at[2], y_up)
        down = both(2)
        ysend[2, lo] = down[:half].astype(BF16)
        send(ysend.at[2, lo], yrecv.at[3], ys_s.at[3], ys_r.at[3], y_down)
        arrived(yrecv.at[0], ys_s.at[0], ys_r.at[0], y_up)
        ysend[1, lo] = (up[:half] + yrecv[0].astype(F32)).astype(BF16)
        send(ysend.at[1, lo], yrecv.at[4], ys_s.at[4], ys_r.at[4], y_up)
        arrived(yrecv.at[1], ys_s.at[1], ys_r.at[1], y_down)
        ysend[2, hi] = (down[half:] + yrecv[1].astype(F32)).astype(BF16)
        send(ysend.at[2, hi], yrecv.at[5], ys_s.at[5], ys_r.at[5], y_down)
        own = both(3)
        for k in range(2, 6):
            arrived(yrecv.at[k], ys_s.at[k], ys_r.at[k], (y_up, y_down)[k % 2])
        low = own[:half] + yrecv[4].astype(F32) + yrecv[3].astype(F32)
        high = own[half:] + yrecv[2].astype(F32) + yrecv[5].astype(F32)
        out_ref[lo, :] = low.astype(BF16)
        out_ref[hi, :] = high.astype(BF16)

    for copy in sends:
        copy.wait_send()


def per_device(
    suffix_x, suffix_z, suffix_b, suffix_c, suffix_dt, missed_x, missed_b, missed_dt,
    dt_bias, a_log, skip_weight_per_head, norm_gain, out_weight, cache_pages,
    hit_holder, hit_slot, missed,
):
    R = lax.axis_size("replica")
    T = lax.axis_size("tensor")
    Z = R // X
    H = Z // 2
    smem = pl.BlockSpec(memory_space=pltpu.SMEM)
    vmem = pl.BlockSpec(memory_space=pltpu.VMEM)
    tokens = REQ * SPAN
    cols = out_weight.shape[1] * R // T
    V = pltpu.VMEM
    D = pltpu.SemaphoreType.DMA
    return pl.pallas_call(
        functools.partial(kernel, Z, T),
        out_shape=jax.ShapeDtypeStruct((tokens, cols), BF16),
        in_specs=[smem] * 4 + [vmem] * 13,
        out_specs=vmem,
        scratch_shapes=[
            pltpu.SMEM((16, 2 * R), jnp.int32),
            pltpu.SMEM((PAGES, 2 * R), jnp.int32),
            V((16, 2 * R), jnp.int32),
            V((PAGES, 2 * R), jnp.int32),
            D((2,)),
            V((R * 64, WIDTH), BF16),
            V((Z, tokens, N), BF16),
            V((3, Z, 2 * ROWS, N), BF16),
            V((4, Z, 2 * ROWS, N), BF16),
            V((2, H, 2 * ROWS, N), BF16),
            V((Z - 1, 2 * X, ROWS, SPAN), BF16),
            V((Z * 2 * X, ROWS, SPAN), BF16),
            V((2 * HEADS, ROWS, SPAN), BF16),
            V((tokens, WIDTH), F32),
            V((tokens, WIDTH), F32),
            V((MISS * SPAN, WIDTH), BF16),
            V((6, SPAN, SPAN), F32),
            V((8, WIDTH), F32),
            V((tokens, WIDTH), BF16),
            D((2, H)), D((2, H)), D((2, H)), D((2, H)),
            D((2, Z)), D((2, Z)), D((2, Z)), D((2, Z)),
            D((NCH, 6)), D((NCH, 6)), D((Z - 1,)), D((Z - 1,)),
            V((4, tokens, cols), BF16),
            V((4, tokens, cols), BF16),
            V((3, tokens, cols), BF16),
            V((6, tokens // 2, cols), BF16),
            D((4,)), D((4,)), D((6,)), D((6,)),
        ],
        compiler_params=pltpu.CompilerParams(
            collective_id=0, has_side_effects=True, vmem_limit_bytes=58 * 1024 * 1024
        ),
        cost_estimate=pl.CostEstimate(
            flops=4 * 10**9, bytes_accessed=8 * 10**6, transcendentals=10**6
        ),
    )(
        missed, dt_bias, a_log, skip_weight_per_head,
        hit_holder[0].transpose(1, 2, 0), hit_slot[0].T, suffix_dt.T, missed_dt.T, norm_gain[None],
        suffix_x, suffix_z, suffix_b, suffix_c, missed_x, missed_b, out_weight.T, cache_pages,
    )


def solution(mesh):
    in_specs = (
        P("replica", "tensor"),
        P("replica", "tensor"),
        P("replica", "tensor"),
        P("replica", "tensor"),
        P("replica", "tensor"),
        P("replica", "tensor"),
        P("replica", "tensor"),
        P("replica", "tensor"),
        P("tensor"),
        P("tensor"),
        P("tensor"),
        P("tensor"),
        P("tensor", "replica"),
        P("replica", "tensor", None, None),
        P("tensor", None, None, None),
        P("tensor", None, None),
        P("replica"),
    )
    return jax.shard_map(
        per_device, mesh=mesh, in_specs=in_specs, out_specs=P("replica", "tensor"), check_vma=False
    )
```

```python
import functools

import jax
import jax.numpy as jnp
from jax import lax
from jax.experimental import pallas as pl
from jax.experimental.pallas import tpu as pltpu
from jax.sharding import PartitionSpec as P

MESH = pl.DeviceIdType.MESH
P_SIZE = 64
N = 256
SPAN = 128
MISS = 3
REQ = 2
HEADS = 16
WIDTH = HEADS * P_SIZE
X = 4
NCH = 4
ROWS = 32
PAGES = 32
F32 = jnp.float32
BF16 = jnp.bfloat16
NT = (((1,), (1,)), ((), ()))
HIGHEST = lax.Precision.HIGHEST


def dot(a, b, precision=None):
    return jnp.dot(a, b, preferred_element_type=F32, precision=precision)


def dot_nt(a, b):
    return lax.dot_general(a, b, NT, preferred_element_type=F32)


def iota(shape, dim):
    return lax.broadcasted_iota(jnp.int32, shape, dim)


def split(v):
    high = v.astype(BF16)
    return jnp.concatenate([high, (v - high.astype(F32)).astype(BF16)], axis=1)


def kernel(
    Z, T,
    missed, bias, a_log, skip, holders, slots, sdt, mdt, gain,
    sx_in, sz_in, sb_in, sc, mx_in, mb_in, w_ref, cache,
    out_ref,
    sx, sz, sb, mx, mb, load_sems, tables, places, tables_v, places_v, table_sems, wt, cg, outp, pg, relay, sp, rp, pt, a0, a1, xs, qs, skips, hid,
    cs, cr, ws, wr, wxs, wxr, wfs, wfr, pgs, pgr, pjs, pjr,
    xsend, xrecv, ysend, yrecv, coresem_s, coresem_r, ys_s, ys_r,
):
    H = Z // 2
    r = lax.axis_index("replica")
    t = lax.axis_index("tensor")
    x = r // Z
    z = r % Z

    def zmod(v):
        return lax.rem(v + Z, Z)

    def at(xx, zz):
        return {"replica": lax.rem(xx + X, X) * Z + zmod(zz), "tensor": t}

    right_x, left_x = at(x + 1, z), at(x - 1, z)
    up_z, down_z = at(x, z + 1), at(x, z - 1)
    peers = [at(x, z + s) for s in range(1, Z)] + [right_x, left_x]
    if T > 1:
        y, c = t // 2, t % 2
        Y = T // 2
        other = {"replica": r, "tensor": y * 2 + 1 - c}
        y_up = {"replica": r, "tensor": lax.rem(y + 1, Y) * 2 + c}
        y_down = {"replica": r, "tensor": lax.rem(y + Y - 1, Y) * 2 + c}
        peers += [other, y_up, y_down]

    loads = [
        pltpu.make_async_copy(src, dst, load_sems.at[k])
        for k, (src, dst) in enumerate(
            ((mx_in, mx), (mb_in, mb), (sx_in, sx), (sb_in, sb), (sz_in, sz))
        )
    ]
    barrier = pltpu.get_barrier_semaphore()
    for peer in peers:
        pl.semaphore_signal(barrier, inc=1, device_id=peer, device_id_type=MESH)

    def w_rows(xx, zz, lo=0, count=64):
        start = (lax.rem(xx + X, X) * Z + zmod(zz)) * 64 + lo
        return wt.at[pl.ds(pl.multiple_of(start, 16), count)]

    wt[pl.ds(pl.multiple_of(r * 64, 16), 64), :] = w_ref[...]
    cg[z] = sc[...]

    requests = holders.shape[2]
    hold = holders[...].reshape(PAGES, requests)
    page_row, request = iota((PAGES, requests), 0), iota((PAGES, requests), 1)
    keys = ((request % REQ) * PAGES + page_row) * 64 + slots[...]
    even = request[0:1] % REQ == 0

    def ends(holder):
        mask = hold == holder
        first = jnp.min(jnp.where(mask, keys, 1 << 20), axis=0, keepdims=True)
        last = jnp.max(jnp.where(mask, keys, -1), axis=0, keepdims=True)
        first = jnp.minimum(first, pltpu.roll(first, requests - 1, 1))
        last = jnp.maximum(last, pltpu.roll(last, requests - 1, 1))
        none = last < 0
        return [jnp.where(none | ~even, 0, first), jnp.where(none | ~even, 0, last)]

    table_rows = [key & 63 for key in ends(r)]
    for offset in (0, X - 1, 1, 2):
        holder = lax.rem(x + offset, X) * Z + z
        table_rows += [(key >= PAGES * 64).astype(jnp.int32) for key in ends(holder)]
    table_rows += [jnp.zeros((1, requests), jnp.int32)] * (16 - len(table_rows))
    for k, row in enumerate(table_rows):
        tables_v[k:k + 1, :] = row

    columns = [
        jnp.sum(jnp.where(request == r * REQ + e, hold, 0), axis=1, keepdims=True) for e in range(REQ)
    ]
    same = page_row == request
    as_rows = [
        jnp.sum(jnp.where(same, jnp.broadcast_to(v, same.shape), 0), axis=0, keepdims=True)
        for v in columns
    ]
    inside, earlier = request < PAGES, request < page_row

    def seen(column, row, mask):
        return jnp.max(jnp.where((column == row) & mask, 1, 0), axis=1, keepdims=True)

    again = [
        seen(columns[0], as_rows[0], earlier),
        jnp.maximum(seen(columns[1], as_rows[0], inside), seen(columns[1], as_rows[1], earlier)),
    ]
    place_table = jnp.zeros((PAGES, requests), jnp.int32)
    for e in range(REQ):
        relative = lax.rem(x + X - columns[e] // Z, X)
        group = jnp.where(relative >= 2, 5 - relative, relative)
        value = (columns[e] % Z) * (2 * X) + group * 2 + again[e]
        place_table = jnp.where(request == e, jnp.broadcast_to(value, same.shape), place_table)
    places_v[...] = place_table
    to_scalars = [
        pltpu.make_async_copy(tables_v, tables, table_sems.at[0]),
        pltpu.make_async_copy(places_v, places, table_sems.at[1]),
    ]
    for copy in to_scalars:
        copy.start()

    def fetch(k, carry):
        zz = zmod(z + (1 - 2 * (k % 2)) * ((k + 1) // 2))
        for g, offset in enumerate((0, 1, X - 1, 2)):
            for s in range(2):
                page = cache[tables[s, (lax.rem(x + offset, X) * Z + zz) * REQ], 0]
                if g == 0:
                    pg[0, k, s * ROWS:(s + 1) * ROWS, :] = page
                else:
                    outp[g - 1, k, s * ROWS:(s + 1) * ROWS, :] = page
        return carry


    sends = []

    def send(src, dst, ssem, rsem, device):
        copy = pltpu.make_async_remote_copy(
            src_ref=src, dst_ref=dst, send_sem=ssem, recv_sem=rsem,
            device_id=device, device_id_type=MESH,
        )
        copy.start()
        sends.append(copy)

    def arrived(ref, ssem, rsem, device):
        pltpu.make_async_remote_copy(
            src_ref=ref, dst_ref=ref, send_sem=ssem, recv_sem=rsem,
            device_id=device, device_id_type=MESH,
        ).wait_recv()

    def c_part(d, step):
        block = zmod(z - step) if d == 0 else zmod(z + step)
        if step < H:
            return cg.at[block]
        return cg.at[block, pl.ds(d * SPAN, SPAN)]

    def c_send(d, step):
        block = zmod(z - step + 1) if d == 0 else zmod(z + step - 1)
        part = cg.at[block] if step < H else cg.at[block, pl.ds(d * SPAN, SPAN)]
        send(part, part, cs.at[d, step - 1], cr.at[d, step - 1], (up_z, down_z)[d])

    def w_part(d, step):
        zz = z - step if d == 0 else z + step
        return w_rows(x, zz) if step < H else w_rows(x, zz, d * 32, 32)

    def w_send(d, step):
        zz = z - step + 1 if d == 0 else z + step - 1
        part = w_rows(x, zz) if step < H else w_rows(x, zz, d * 32, 32)
        send(part, part, ws.at[d, step - 1], wr.at[d, step - 1], (up_z, down_z)[d])

    def z_of(k):
        if k == 0:
            return z
        step = (k + 1) // 2
        return z - step if k % 2 == 1 else z + step

    def wx_send(k):
        part = w_rows(x, z_of(k))
        send(part, part, wxs.at[0, k], wxr.at[0, k], right_x)
        send(part, part, wxs.at[1, k], wxr.at[1, k], left_x)

    def wx_pass(k):
        arrived(w_rows(x - 1, z_of(k)), wxs.at[0, k], wxr.at[0, k], right_x)
        part = w_rows(x - 1, z_of(k), 0, 32)
        send(part, part, wfs.at[0, k], wfr.at[0, k], right_x)
        arrived(w_rows(x + 1, z_of(k)), wxs.at[1, k], wxr.at[1, k], left_x)
        part = w_rows(x + 1, z_of(k), 32, 32)
        send(part, part, wfs.at[1, k], wfr.at[1, k], left_x)

    for load in loads:
        load.start()
    pl.semaphore_wait(barrier, len(peers))
    c_send(0, 1)
    c_send(1, 1)
    w_send(0, 1)
    w_send(1, 1)
    for copy in to_scalars:
        copy.wait()
    CHUNK = Z // NCH
    HALF = CHUNK // 2
    for chunk in range(NCH):
        lax.fori_loop(chunk * CHUNK, (chunk + 1) * CHUNK, fetch, 0)
        whole = pl.ds(chunk * CHUNK, CHUNK)
        first, second = pl.ds(chunk * CHUNK, HALF), pl.ds(chunk * CHUNK + HALF, HALF)
        via = pl.ds(chunk * HALF, HALF)
        ss, rs = [pgs.at[chunk, k] for k in range(6)], [pgr.at[chunk, k] for k in range(6)]
        send(outp.at[2, first], relay.at[0, via], ss[0], rs[0], right_x)
        send(outp.at[2, second], relay.at[1, via], ss[1], rs[1], left_x)
        send(outp.at[0, whole], pg.at[1, whole], ss[2], rs[2], right_x)
        send(outp.at[1, whole], pg.at[2, whole], ss[3], rs[3], left_x)

    def pages_pass(chunk):
        first, second = pl.ds(chunk * CHUNK, HALF), pl.ds(chunk * CHUNK + HALF, HALF)
        via = pl.ds(chunk * HALF, HALF)
        ss, rs = [pgs.at[chunk, k] for k in range(6)], [pgr.at[chunk, k] for k in range(6)]
        arrived(relay.at[0, via], ss[0], rs[0], right_x)
        send(relay.at[0, via], pg.at[3, first], ss[4], rs[4], right_x)
        arrived(relay.at[1, via], ss[1], rs[1], left_x)
        send(relay.at[1, via], pg.at[3, second], ss[5], rs[5], left_x)

    def pages_wait(chunk):
        whole = pl.ds(chunk * CHUNK, CHUNK)
        first, second = pl.ds(chunk * CHUNK, HALF), pl.ds(chunk * CHUNK + HALF, HALF)
        ss, rs = [pgs.at[chunk, k] for k in range(6)], [pgr.at[chunk, k] for k in range(6)]
        arrived(pg.at[1, whole], ss[2], rs[2], right_x)
        arrived(pg.at[2, whole], ss[3], rs[3], left_x)
        arrived(pg.at[3, first], ss[4], rs[4], right_x)
        arrived(pg.at[3, second], ss[5], rs[5], left_x)

    def rp_of(zz):
        return rp.at[pl.ds(zz * 2 * X, 2 * X)]

    waited = set()

    def project(k):
        if k // CHUNK not in waited:
            waited.add(k // CHUNK)
            pages_wait(k // CHUNK)
        dz = zmod(z_of(k))
        pages = jnp.concatenate([pg[g, k] for g in range(4)], axis=0)
        full = dot_nt(pages, cg[dz])
        parts = []
        for slot in range(8):
            second = tables[2 + slot, (x * Z + dz) * REQ].astype(F32)
            rows = full[slot * ROWS:(slot + 1) * ROWS]
            parts.append(rows[:, :SPAN] * (1.0 - second) + rows[:, SPAN:] * second)
        products = jnp.stack(parts).astype(BF16)
        if k == 0:
            rp[pl.ds(z * 2 * X, 2 * X)] = products
        else:
            sp[k - 1] = products
            send(sp.at[k - 1], rp_of(z), pjs.at[k - 1], pjr.at[k - 1], at(x, dz))

    lane = iota((1, SPAN), 1)
    lane_block = (lane // HEADS) % 4

    def per_head(scalars):
        row = jnp.zeros((1, SPAN), F32)
        for h in range(HEADS):
            row = jnp.where(lane % HEADS == h, scalars[h], row)
        return row

    def decays():
        for load in loads:
            load.wait()
        rows, cols = iota((SPAN, SPAN), 0), iota((SPAN, SPAN), 1)
        first = lane < 64
        count = jnp.where(first, missed[0], missed[1])
        active = jnp.where(lane_block == 3, 1, (lane_block >= MISS - count).astype(jnp.int32))
        active = active.astype(F32)
        steps = []
        for q_ in range(REQ):
            steps += [mdt[:, (q_ * MISS + b) * SPAN:(q_ * MISS + b + 1) * SPAN] for b in range(MISS)]
            steps.append(sdt[:, q_ * SPAN:(q_ + 1) * SPAN])
        raw = jnp.concatenate(steps, axis=0).T + per_head(bias)
        dt = jnp.maximum(raw, 0.0) + jnp.log1p(jnp.exp(-jnp.abs(raw)))
        dt = dt * active
        q = dot((rows >= cols).astype(F32), -jnp.exp(per_head(a_log)) * dt, HIGHEST)
        row_block, col_block = (rows // HEADS) % 4, (cols // HEADS) % 4
        later = (row_block < 3) & ((row_block >= col_block) | (col_block == 3))
        same = (rows // 64 == cols // 64) & (rows % HEADS == cols % HEADS)
        last = jnp.broadcast_to(q[SPAN - 1:, :], (8, SPAN))
        tail = dot(last, (later & same).astype(F32), HIGHEST)[0:1]
        weight = jnp.exp(jnp.where(lane_block == 3, q, tail - q))
        weight = jnp.where(lane_block == 3, weight, weight * dt)
        qs[0] = q
        qs[1] = q.T
        qs[2] = dt.T
        qs[3] = weight
        qs[4] = jnp.exp(jnp.where(lane_block == 3, q + tail, 0.0))
        skips[...] = spread(jnp.broadcast_to(per_head(skip), (8, SPAN)), 0)

    def spread(values, block):
        chosen = jnp.where(lane // HEADS == block, values, 0.0)
        heads = iota((2 * SPAN, WIDTH), 0) % HEADS
        picked = (heads == iota((2 * SPAN, WIDTH), 1) // P_SIZE).astype(BF16)
        return dot(split(chosen), picked)

    def missed_block(q_, b):
        weight = spread(qs[3], q_ * 4 + b)
        at_ = (q_ * MISS + b) * SPAN
        xs[b * SPAN:(b + 1) * SPAN, :] = (mx[at_:at_ + SPAN, :].astype(F32) * weight).astype(BF16)

    def carried(q_):
        rows = slice(q_ * SPAN, (q_ + 1) * SPAN)
        scores = dot_nt(sc[rows, :], mb[q_ * MISS * SPAN:(q_ + 1) * MISS * SPAN, :])
        rest = dot(scores.astype(BF16), xs[...])
        a0[rows, :] = rest * spread(qs[3], q_ * 4 + 3) + skips[0:1, :] * sx[rows, :].astype(F32)
        qs[5] = dot_nt(sc[rows, :], sb[rows, :])

    def pair(q_, p):
        rows = slice(q_ * SPAN, (q_ + 1) * SPAN)
        cols = slice(p * 2 * P_SIZE, (p + 1) * 2 * P_SIZE)
        causal = iota((SPAN, SPAN), 0) >= iota((SPAN, SPAN), 1)
        mixes = []
        for h in range(2):
            at_ = q_ * 64 + 48 + p * 2 + h
            gap = jnp.where(causal, qs[0, :, at_:at_ + 1] - qs[1, at_:at_ + 1, :], -jnp.inf)
            mixes.append((jnp.exp(gap) * qs[2, at_:at_ + 1, :] * qs[5]).astype(BF16))
        two = sx[rows, cols]
        low = iota((SPAN, 2 * P_SIZE), 1) < P_SIZE
        zero = jnp.zeros_like(two)
        stacked = jnp.concatenate([jnp.where(low, two, zero), jnp.where(low, zero, two)], axis=0)
        a0[rows, cols] += dot(jnp.concatenate(mixes, axis=1), stacked)

    def gates(q_):
        rows = slice(q_ * SPAN, (q_ + 1) * SPAN)
        v = sz[rows, :].astype(F32)
        gate = v / (1.0 + jnp.exp(-v))
        a0[rows, :] = a0[rows, :] * gate
        a1[rows, :] = spread(qs[4], q_ * 4 + 3) * gate

    work = [decays]
    for q_ in range(REQ):
        work += [functools.partial(missed_block, q_, b) for b in range(MISS)]
        work.append(functools.partial(carried, q_))
        work += [functools.partial(pair, q_, p) for p in range(HEADS // 2)]
        work.append(functools.partial(gates, q_))

    share = -(-len(work) // H)
    projected, moved, passed = 1, 0, 0
    for i in range(1, H + 1):
        for d in range(2):
            arrived(c_part(d, i), cs.at[d, i - 1], cr.at[d, i - 1], (up_z, down_z)[d])
            if i < H:
                c_send(d, i + 1)
        for d in range(2):
            arrived(w_part(d, i), ws.at[d, i - 1], wr.at[d, i - 1], (up_z, down_z)[d])
            if i < H:
                w_send(d, i + 1)
        while i >= 3 and moved < min(2 * i + 1, Z):
            wx_send(moved)
            moved += 1
        if 2 <= i < 2 + NCH:
            pages_pass(i - 2)
        for _ in range(8 if i >= 7 else 0):
            if projected < min(2 * i + 1, Z):
                project(projected)
                projected += 1
        for _ in range({7: 2, 8: 1}.get(i, 0)):
            wx_pass(passed)
            passed += 1
        for _ in range(share):
            if work:
                work.pop(0)()
    for chunk in range(max(0, H - 1), NCH):
        pages_pass(chunk)
    while projected < Z:
        project(projected)
        projected += 1
    project(0)
    while passed < Z:
        wx_pass(passed)
        passed += 1
    for k in range(1, Z):
        arrived(rp_of(zmod(2 * z - z_of(k))), pjs.at[k - 1], pjr.at[k - 1], up_z)

    eye = (iota((SPAN, SPAN), 0) == iota((SPAN, SPAN), 1)).astype(BF16)
    for q_ in range(REQ):
        def place(j, carry, q_=q_):
            pt[j] = rp[places[j, q_]]
            return carry

        lax.fori_loop(0, 2 * HEADS, place, 0, unroll=8)
        rows = slice(q_ * SPAN, (q_ + 1) * SPAN)
        g = a0[rows, :] + a1[rows, :] * dot_nt(eye, pt[...].reshape(WIDTH, SPAN))
        scale = lax.rsqrt(jnp.mean(g * g, axis=-1, keepdims=True) + 1e-05)
        hid[rows, :] = (g * scale * gain[...]).astype(BF16)

    for k in range(Z):
        arrived(w_rows(x + 2, z_of(k), 0, 32), wfs.at[0, k], wfr.at[0, k], right_x)
        arrived(w_rows(x + 2, z_of(k), 32, 32), wfs.at[1, k], wfr.at[1, k], left_x)

    cols = out_ref.shape[1]

    def product(block):
        weights = wt[pl.ds(pl.multiple_of(block * cols, cols), cols), :]
        return dot_nt(hid[...], weights)

    if T == 1:
        out_ref[...] = product(0).astype(BF16)
    else:
        offsets = (2, 1, Y - 1, 0)

        def block_of(k, core):
            return lax.rem(y + offsets[k], Y) * 2 + core

        for k in range(4):
            xsend[k] = product(block_of(k, 1 - c)).astype(BF16)
            send(xsend.at[k], xrecv.at[k], coresem_s.at[k], coresem_r.at[k], other)

        def both(k):
            mine = product(block_of(k, c))
            arrived(xrecv.at[k], coresem_s.at[k], coresem_r.at[k], other)
            return mine + xrecv[k].astype(F32)

        half = out_ref.shape[0] // 2
        lo, hi = pl.ds(0, half), pl.ds(half, half)
        ysend[0] = both(0).astype(BF16)
        send(ysend.at[0, lo], yrecv.at[0], ys_s.at[0], ys_r.at[0], y_up)
        send(ysend.at[0, hi], yrecv.at[1], ys_s.at[1], ys_r.at[1], y_down)
        up = both(1)
        ysend[1, hi] = up[half:].astype(BF16)
        send(ysend.at[1, hi], yrecv.at[2], ys_s.at[2], ys_r.at[2], y_up)
        down = both(2)
        ysend[2, lo] = down[:half].astype(BF16)
        send(ysend.at[2, lo], yrecv.at[3], ys_s.at[3], ys_r.at[3], y_down)
        arrived(yrecv.at[0], ys_s.at[0], ys_r.at[0], y_up)
        ysend[1, lo] = (up[:half] + yrecv[0].astype(F32)).astype(BF16)
        send(ysend.at[1, lo], yrecv.at[4], ys_s.at[4], ys_r.at[4], y_up)
        arrived(yrecv.at[1], ys_s.at[1], ys_r.at[1], y_down)
        ysend[2, hi] = (down[half:] + yrecv[1].astype(F32)).astype(BF16)
        send(ysend.at[2, hi], yrecv.at[5], ys_s.at[5], ys_r.at[5], y_down)
        own = both(3)
        for k in range(2, 6):
            arrived(yrecv.at[k], ys_s.at[k], ys_r.at[k], (y_up, y_down)[k % 2])
        low = own[:half] + yrecv[4].astype(F32) + yrecv[3].astype(F32)
        high = own[half:] + yrecv[2].astype(F32) + yrecv[5].astype(F32)
        out_ref[lo, :] = low.astype(BF16)
        out_ref[hi, :] = high.astype(BF16)

    for copy in sends:
        copy.wait_send()


def per_device(
    suffix_x, suffix_z, suffix_b, suffix_c, suffix_dt, missed_x, missed_b, missed_dt,
    dt_bias, a_log, skip_weight_per_head, norm_gain, out_weight, cache_pages,
    hit_holder, hit_slot, missed,
):
    R = lax.axis_size("replica")
    T = lax.axis_size("tensor")
    Z = R // X
    H = Z // 2
    smem = pl.BlockSpec(memory_space=pltpu.SMEM)
    vmem = pl.BlockSpec(memory_space=pltpu.VMEM)
    hbm = pl.BlockSpec(memory_space=pl.ANY)
    tokens = REQ * SPAN
    cols = out_weight.shape[1] * R // T
    V = pltpu.VMEM
    D = pltpu.SemaphoreType.DMA
    return pl.pallas_call(
        functools.partial(kernel, Z, T),
        out_shape=jax.ShapeDtypeStruct((tokens, cols), BF16),
        in_specs=[smem] * 4 + [vmem] * 5 + [hbm] * 3 + [vmem] + [hbm] * 2 + [vmem] * 2,
        out_specs=vmem,
        scratch_shapes=[
            V((tokens, WIDTH), BF16),
            V((tokens, WIDTH), BF16),
            V((tokens, N), BF16),
            V((MISS * tokens, WIDTH), BF16),
            V((MISS * tokens, N), BF16),
            D((5,)),
            pltpu.SMEM((16, 2 * R), jnp.int32),
            pltpu.SMEM((PAGES, 2 * R), jnp.int32),
            V((16, 2 * R), jnp.int32),
            V((PAGES, 2 * R), jnp.int32),
            D((2,)),
            V((R * 64, WIDTH), BF16),
            V((Z, tokens, N), BF16),
            V((3, Z, 2 * ROWS, N), BF16),
            V((4, Z, 2 * ROWS, N), BF16),
            V((2, H, 2 * ROWS, N), BF16),
            V((Z - 1, 2 * X, ROWS, SPAN), BF16),
            V((Z * 2 * X, ROWS, SPAN), BF16),
            V((2 * HEADS, ROWS, SPAN), BF16),
            V((tokens, WIDTH), F32),
            V((tokens, WIDTH), F32),
            V((MISS * SPAN, WIDTH), BF16),
            V((6, SPAN, SPAN), F32),
            V((8, WIDTH), F32),
            V((tokens, WIDTH), BF16),
            D((2, H)), D((2, H)), D((2, H)), D((2, H)),
            D((2, Z)), D((2, Z)), D((2, Z)), D((2, Z)),
            D((NCH, 6)), D((NCH, 6)), D((Z - 1,)), D((Z - 1,)),
            V((4, tokens, cols), BF16),
            V((4, tokens, cols), BF16),
            V((3, tokens, cols), BF16),
            V((6, tokens // 2, cols), BF16),
            D((4,)), D((4,)), D((6,)), D((6,)),
        ],
        compiler_params=pltpu.CompilerParams(
            collective_id=0, has_side_effects=True, vmem_limit_bytes=58 * 1024 * 1024
        ),
        cost_estimate=pl.CostEstimate(
            flops=4 * 10**9, bytes_accessed=8 * 10**6, transcendentals=10**6
        ),
    )(
        missed, dt_bias, a_log, skip_weight_per_head,
        hit_holder[0].transpose(1, 2, 0), hit_slot[0].T, suffix_dt.T, missed_dt.T, norm_gain[None],
        suffix_x, suffix_z, suffix_b, suffix_c, missed_x, missed_b, out_weight.T, cache_pages,
    )


def solution(mesh):
    in_specs = (
        P("replica", "tensor"),
        P("replica", "tensor"),
        P("replica", "tensor"),
        P("replica", "tensor"),
        P("replica", "tensor"),
        P("replica", "tensor"),
        P("replica", "tensor"),
        P("replica", "tensor"),
        P("tensor"),
        P("tensor"),
        P("tensor"),
        P("tensor"),
        P("tensor", "replica"),
        P("replica", "tensor", None, None),
        P("tensor", None, None, None),
        P("tensor", None, None),
        P("replica"),
    )
    return jax.shard_map(
        per_device, mesh=mesh, in_specs=in_specs, out_specs=P("replica", "tensor"), check_vma=False
    )
```

```python
import functools

import jax
import jax.numpy as jnp
from jax import lax
from jax.experimental import pallas as pl
from jax.experimental.pallas import tpu as pltpu
from jax.sharding import PartitionSpec as P

MESH = pl.DeviceIdType.MESH
P_SIZE = 64
N = 256
SPAN = 128
MISS = 3
REQ = 2
HEADS = 16
WIDTH = HEADS * P_SIZE
X = 4
NCH = 4
ROWS = 32
PAGES = 32
F32 = jnp.float32
BF16 = jnp.bfloat16
NT = (((1,), (1,)), ((), ()))
HIGHEST = lax.Precision.HIGHEST


def dot(a, b, precision=None):
    return jnp.dot(a, b, preferred_element_type=F32, precision=precision)


def dot_nt(a, b):
    return lax.dot_general(a, b, NT, preferred_element_type=F32)


def iota(shape, dim):
    return lax.broadcasted_iota(jnp.int32, shape, dim)


def split(v):
    high = v.astype(BF16)
    return jnp.concatenate([high, (v - high.astype(F32)).astype(BF16)], axis=1)


def kernel(
    Z, T,
    missed, bias, a_log, skip, holders, slots, sdt, mdt, gain,
    sx_in, sz_in, sb_in, sc, mx_in, mb_in, w_ref, cache,
    out_ref,
    sx, sz, sb, mx, mb, load_sems, tables, places, tables_v, places_v, table_sems, wt, cg, outp, pg, relay, sp, rp, pt, a0, a1, xs, qs, skips, hid, mid, mids, midr,
    cs, cr, ws, wr, wxs, wxr, wfs, wfr, pgs, pgr, pjs, pjr,
    xsend, xrecv, ysend, yrecv, coresem_s, coresem_r, ys_s, ys_r,
):
    H = Z // 2
    r = lax.axis_index("replica")
    t = lax.axis_index("tensor")
    x = r // Z
    z = r % Z

    def zmod(v):
        return lax.rem(v + Z, Z)

    def at(xx, zz):
        return {"replica": lax.rem(xx + X, X) * Z + zmod(zz), "tensor": t}

    right_x, left_x = at(x + 1, z), at(x - 1, z)
    up_z, down_z = at(x, z + 1), at(x, z - 1)
    peers = [at(x, z + s) for s in range(1, Z)] + [right_x, left_x]
    if T > 1:
        y, c = t // 2, t % 2
        Y = T // 2
        other = {"replica": r, "tensor": y * 2 + 1 - c}
        y_up = {"replica": r, "tensor": lax.rem(y + 1, Y) * 2 + c}
        y_down = {"replica": r, "tensor": lax.rem(y + Y - 1, Y) * 2 + c}
        peers += [other, y_up, y_down]

    loads = [
        pltpu.make_async_copy(src, dst, load_sems.at[k])
        for k, (src, dst) in enumerate(
            ((mx_in, mx), (mb_in, mb), (sx_in, sx), (sb_in, sb), (sz_in, sz))
        )
    ]
    barrier = pltpu.get_barrier_semaphore()
    for peer in peers:
        pl.semaphore_signal(barrier, inc=1, device_id=peer, device_id_type=MESH)

    def w_rows(xx, zz, lo=0, count=64):
        start = (lax.rem(xx + X, X) * Z + zmod(zz)) * 64 + lo
        return wt.at[pl.ds(pl.multiple_of(start, 16), count)]

    wt[pl.ds(pl.multiple_of(r * 64, 16), 64), :] = w_ref[...]
    cg[z] = sc[...]

    requests = holders.shape[2]
    hold = holders[...].reshape(PAGES, requests)
    page_row, request = iota((PAGES, requests), 0), iota((PAGES, requests), 1)
    keys = ((request % REQ) * PAGES + page_row) * 64 + slots[...]
    even = request[0:1] % REQ == 0

    def ends(holder):
        mask = hold == holder
        first = jnp.min(jnp.where(mask, keys, 1 << 20), axis=0, keepdims=True)
        last = jnp.max(jnp.where(mask, keys, -1), axis=0, keepdims=True)
        first = jnp.minimum(first, pltpu.roll(first, requests - 1, 1))
        last = jnp.maximum(last, pltpu.roll(last, requests - 1, 1))
        none = last < 0
        return [jnp.where(none | ~even, 0, first), jnp.where(none | ~even, 0, last)]

    table_rows = [key & 63 for key in ends(r)]
    for offset in (0, X - 1, 1, 2):
        holder = lax.rem(x + offset, X) * Z + z
        table_rows += [(key >= PAGES * 64).astype(jnp.int32) for key in ends(holder)]
    table_rows += [jnp.zeros((1, requests), jnp.int32)] * (16 - len(table_rows))
    for k, row in enumerate(table_rows):
        tables_v[k:k + 1, :] = row

    columns = [
        jnp.sum(jnp.where(request == r * REQ + e, hold, 0), axis=1, keepdims=True) for e in range(REQ)
    ]
    same = page_row == request
    as_rows = [
        jnp.sum(jnp.where(same, jnp.broadcast_to(v, same.shape), 0), axis=0, keepdims=True)
        for v in columns
    ]
    inside, earlier = request < PAGES, request < page_row

    def seen(column, row, mask):
        return jnp.max(jnp.where((column == row) & mask, 1, 0), axis=1, keepdims=True)

    again = [
        seen(columns[0], as_rows[0], earlier),
        jnp.maximum(seen(columns[1], as_rows[0], inside), seen(columns[1], as_rows[1], earlier)),
    ]
    place_table = jnp.zeros((PAGES, requests), jnp.int32)
    for e in range(REQ):
        relative = lax.rem(x + X - columns[e] // Z, X)
        group = jnp.where(relative >= 2, 5 - relative, relative)
        value = (columns[e] % Z) * (2 * X) + group * 2 + again[e]
        place_table = jnp.where(request == e, jnp.broadcast_to(value, same.shape), place_table)
    places_v[...] = place_table
    to_scalars = [
        pltpu.make_async_copy(tables_v, tables, table_sems.at[0]),
        pltpu.make_async_copy(places_v, places, table_sems.at[1]),
    ]
    for copy in to_scalars:
        copy.start()

    def fetch(k, carry):
        zz = zmod(z + (1 - 2 * (k % 2)) * ((k + 1) // 2))
        for g, offset in enumerate((0, 1, X - 1, 2)):
            for s in range(2):
                page = cache[tables[s, (lax.rem(x + offset, X) * Z + zz) * REQ], 0]
                if g == 0:
                    pg[0, k, s * ROWS:(s + 1) * ROWS, :] = page
                else:
                    outp[g - 1, k, s * ROWS:(s + 1) * ROWS, :] = page
        return carry


    sends = []

    def send(src, dst, ssem, rsem, device):
        copy = pltpu.make_async_remote_copy(
            src_ref=src, dst_ref=dst, send_sem=ssem, recv_sem=rsem,
            device_id=device, device_id_type=MESH,
        )
        copy.start()
        sends.append(copy)

    def arrived(ref, ssem, rsem, device):
        pltpu.make_async_remote_copy(
            src_ref=ref, dst_ref=ref, send_sem=ssem, recv_sem=rsem,
            device_id=device, device_id_type=MESH,
        ).wait_recv()

    def c_part(d, step):
        block = zmod(z - step) if d == 0 else zmod(z + step)
        if step < H:
            return cg.at[block]
        return cg.at[block, pl.ds(d * SPAN, SPAN)]

    def c_send(d, step):
        block = zmod(z - step + 1) if d == 0 else zmod(z + step - 1)
        part = cg.at[block] if step < H else cg.at[block, pl.ds(d * SPAN, SPAN)]
        send(part, part, cs.at[d, step - 1], cr.at[d, step - 1], (up_z, down_z)[d])

    def w_part(d, step):
        zz = z - step if d == 0 else z + step
        return w_rows(x, zz) if step < H else w_rows(x, zz, d * 32, 32)

    def w_send(d, step):
        zz = z - step + 1 if d == 0 else z + step - 1
        part = w_rows(x, zz) if step < H else w_rows(x, zz, d * 32, 32)
        send(part, part, ws.at[d, step - 1], wr.at[d, step - 1], (up_z, down_z)[d])

    def z_of(k):
        if k == 0:
            return z
        step = (k + 1) // 2
        return z - step if k % 2 == 1 else z + step

    def wx_send(k):
        part = w_rows(x, z_of(k))
        send(part, part, wxs.at[0, k], wxr.at[0, k], right_x)
        send(part, part, wxs.at[1, k], wxr.at[1, k], left_x)

    def wx_pass(k):
        arrived(w_rows(x - 1, z_of(k)), wxs.at[0, k], wxr.at[0, k], right_x)
        part = w_rows(x - 1, z_of(k), 0, 32)
        send(part, part, wfs.at[0, k], wfr.at[0, k], right_x)
        arrived(w_rows(x + 1, z_of(k)), wxs.at[1, k], wxr.at[1, k], left_x)
        part = w_rows(x + 1, z_of(k), 32, 32)
        send(part, part, wfs.at[1, k], wfr.at[1, k], left_x)

    for load in loads:
        load.start()
    pl.semaphore_wait(barrier, len(peers))
    c_send(0, 1)
    c_send(1, 1)
    w_send(0, 1)
    w_send(1, 1)
    for copy in to_scalars:
        copy.wait()
    CHUNK = Z // NCH
    HALF = CHUNK // 2
    for chunk in range(NCH):
        lax.fori_loop(chunk * CHUNK, (chunk + 1) * CHUNK, fetch, 0)
        whole = pl.ds(chunk * CHUNK, CHUNK)
        first, second = pl.ds(chunk * CHUNK, HALF), pl.ds(chunk * CHUNK + HALF, HALF)
        via = pl.ds(chunk * HALF, HALF)
        ss, rs = [pgs.at[chunk, k] for k in range(6)], [pgr.at[chunk, k] for k in range(6)]
        send(outp.at[2, first], relay.at[0, via], ss[0], rs[0], right_x)
        send(outp.at[2, second], relay.at[1, via], ss[1], rs[1], left_x)
        send(outp.at[0, whole], pg.at[1, whole], ss[2], rs[2], right_x)
        send(outp.at[1, whole], pg.at[2, whole], ss[3], rs[3], left_x)

    def pages_pass(chunk):
        first, second = pl.ds(chunk * CHUNK, HALF), pl.ds(chunk * CHUNK + HALF, HALF)
        via = pl.ds(chunk * HALF, HALF)
        ss, rs = [pgs.at[chunk, k] for k in range(6)], [pgr.at[chunk, k] for k in range(6)]
        arrived(relay.at[0, via], ss[0], rs[0], right_x)
        send(relay.at[0, via], pg.at[3, first], ss[4], rs[4], right_x)
        arrived(relay.at[1, via], ss[1], rs[1], left_x)
        send(relay.at[1, via], pg.at[3, second], ss[5], rs[5], left_x)

    def pages_wait(chunk):
        whole = pl.ds(chunk * CHUNK, CHUNK)
        first, second = pl.ds(chunk * CHUNK, HALF), pl.ds(chunk * CHUNK + HALF, HALF)
        ss, rs = [pgs.at[chunk, k] for k in range(6)], [pgr.at[chunk, k] for k in range(6)]
        arrived(pg.at[1, whole], ss[2], rs[2], right_x)
        arrived(pg.at[2, whole], ss[3], rs[3], left_x)
        arrived(pg.at[3, first], ss[4], rs[4], right_x)
        arrived(pg.at[3, second], ss[5], rs[5], left_x)

    def rp_of(zz):
        return rp.at[pl.ds(zz * 2 * X, 2 * X)]

    waited = set()

    def project(k):
        if k // CHUNK not in waited:
            waited.add(k // CHUNK)
            pages_wait(k // CHUNK)
        dz = zmod(z_of(k))
        pages = jnp.concatenate([pg[g, k] for g in range(4)], axis=0)
        full = dot_nt(pages, cg[dz])
        parts = []
        for slot in range(8):
            second = tables[2 + slot, (x * Z + dz) * REQ].astype(F32)
            rows = full[slot * ROWS:(slot + 1) * ROWS]
            parts.append(rows[:, :SPAN] * (1.0 - second) + rows[:, SPAN:] * second)
        products = jnp.stack(parts).astype(BF16)
        if k == 0:
            rp[pl.ds(z * 2 * X, 2 * X)] = products
        elif k == Z - 1:
            sp[k - 1] = products
            send(sp.at[k - 1, pl.ds(0, X)], mid.at[0], mids.at[0], midr.at[0], at(x, z - H // 2))
            send(sp.at[k - 1, pl.ds(X, X)], mid.at[1], mids.at[1], midr.at[1], at(x, z + H // 2))
        else:
            sp[k - 1] = products
            send(sp.at[k - 1], rp_of(z), pjs.at[k - 1], pjr.at[k - 1], at(x, dz))

    def rp_half(zz, d):
        return rp.at[pl.ds(zmod(zz) * 2 * X + d * X, X)]

    def far_pass():
        below, above = at(x, z - H // 2), at(x, z + H // 2)
        arrived(mid.at[0], mids.at[0], midr.at[0], below)
        send(mid.at[0], rp_half(z + H // 2, 0), mids.at[2], midr.at[2], below)
        arrived(mid.at[1], mids.at[1], midr.at[1], above)
        send(mid.at[1], rp_half(z - H // 2, 1), mids.at[3], midr.at[3], above)

    lane = iota((1, SPAN), 1)
    lane_block = (lane // HEADS) % 4

    def per_head(scalars):
        row = jnp.zeros((1, SPAN), F32)
        for h in range(HEADS):
            row = jnp.where(lane % HEADS == h, scalars[h], row)
        return row

    def decays():
        for load in loads:
            load.wait()
        rows, cols = iota((SPAN, SPAN), 0), iota((SPAN, SPAN), 1)
        first = lane < 64
        count = jnp.where(first, missed[0], missed[1])
        active = jnp.where(lane_block == 3, 1, (lane_block >= MISS - count).astype(jnp.int32))
        active = active.astype(F32)
        steps = []
        for q_ in range(REQ):
            steps += [mdt[:, (q_ * MISS + b) * SPAN:(q_ * MISS + b + 1) * SPAN] for b in range(MISS)]
            steps.append(sdt[:, q_ * SPAN:(q_ + 1) * SPAN])
        raw = jnp.concatenate(steps, axis=0).T + per_head(bias)
        dt = jnp.maximum(raw, 0.0) + jnp.log1p(jnp.exp(-jnp.abs(raw)))
        dt = dt * active
        q = dot((rows >= cols).astype(F32), -jnp.exp(per_head(a_log)) * dt, HIGHEST)
        row_block, col_block = (rows // HEADS) % 4, (cols // HEADS) % 4
        later = (row_block < 3) & ((row_block >= col_block) | (col_block == 3))
        same = (rows // 64 == cols // 64) & (rows % HEADS == cols % HEADS)
        last = jnp.broadcast_to(q[SPAN - 1:, :], (8, SPAN))
        tail = dot(last, (later & same).astype(F32), HIGHEST)[0:1]
        weight = jnp.exp(jnp.where(lane_block == 3, q, tail - q))
        weight = jnp.where(lane_block == 3, weight, weight * dt)
        qs[0] = q
        qs[1] = q.T
        qs[2] = dt.T
        qs[3] = weight
        qs[4] = jnp.exp(jnp.where(lane_block == 3, q + tail, 0.0))
        skips[...] = spread(jnp.broadcast_to(per_head(skip), (8, SPAN)), 0)

    def spread(values, block):
        chosen = jnp.where(lane // HEADS == block, values, 0.0)
        heads = iota((2 * SPAN, WIDTH), 0) % HEADS
        picked = (heads == iota((2 * SPAN, WIDTH), 1) // P_SIZE).astype(BF16)
        return dot(split(chosen), picked)

    def missed_block(q_, b):
        weight = spread(qs[3], q_ * 4 + b)
        at_ = (q_ * MISS + b) * SPAN
        xs[b * SPAN:(b + 1) * SPAN, :] = (mx[at_:at_ + SPAN, :].astype(F32) * weight).astype(BF16)

    def carried(q_):
        rows = slice(q_ * SPAN, (q_ + 1) * SPAN)
        scores = dot_nt(sc[rows, :], mb[q_ * MISS * SPAN:(q_ + 1) * MISS * SPAN, :])
        rest = dot(scores.astype(BF16), xs[...])
        a0[rows, :] = rest * spread(qs[3], q_ * 4 + 3) + skips[0:1, :] * sx[rows, :].astype(F32)
        qs[5] = dot_nt(sc[rows, :], sb[rows, :])

    def pair(q_, p):
        rows = slice(q_ * SPAN, (q_ + 1) * SPAN)
        cols = slice(p * 2 * P_SIZE, (p + 1) * 2 * P_SIZE)
        causal = iota((SPAN, SPAN), 0) >= iota((SPAN, SPAN), 1)
        mixes = []
        for h in range(2):
            at_ = q_ * 64 + 48 + p * 2 + h
            gap = jnp.where(causal, qs[0, :, at_:at_ + 1] - qs[1, at_:at_ + 1, :], -jnp.inf)
            mixes.append((jnp.exp(gap) * qs[2, at_:at_ + 1, :] * qs[5]).astype(BF16))
        two = sx[rows, cols]
        low = iota((SPAN, 2 * P_SIZE), 1) < P_SIZE
        zero = jnp.zeros_like(two)
        stacked = jnp.concatenate([jnp.where(low, two, zero), jnp.where(low, zero, two)], axis=0)
        a0[rows, cols] += dot(jnp.concatenate(mixes, axis=1), stacked)

    def gates(q_):
        rows = slice(q_ * SPAN, (q_ + 1) * SPAN)
        v = sz[rows, :].astype(F32)
        gate = v / (1.0 + jnp.exp(-v))
        a0[rows, :] = a0[rows, :] * gate
        a1[rows, :] = spread(qs[4], q_ * 4 + 3) * gate

    work = [decays]
    for q_ in range(REQ):
        work += [functools.partial(missed_block, q_, b) for b in range(MISS)]
        work.append(functools.partial(carried, q_))
        work += [functools.partial(pair, q_, p) for p in range(HEADS // 2)]
        work.append(functools.partial(gates, q_))

    share = -(-len(work) // H)
    projected, moved, passed = 1, 0, 0
    for i in range(1, H + 1):
        for d in range(2):
            arrived(c_part(d, i), cs.at[d, i - 1], cr.at[d, i - 1], (up_z, down_z)[d])
            if i < H:
                c_send(d, i + 1)
        for d in range(2):
            arrived(w_part(d, i), ws.at[d, i - 1], wr.at[d, i - 1], (up_z, down_z)[d])
            if i < H:
                w_send(d, i + 1)
        while i >= 3 and moved < min(2 * i + 1, Z):
            wx_send(moved)
            moved += 1
        if 2 <= i < 2 + NCH:
            pages_pass(i - 2)
        if i == H:
            project(Z - 1)
        for _ in range(8 if i >= H - 1 else 0):
            if projected < min(2 * i + 1, Z - 1):
                project(projected)
                projected += 1
        for _ in range({7: 2, 8: 1}.get(i, 0)):
            wx_pass(passed)
            passed += 1
        for _ in range(share):
            if work:
                work.pop(0)()
    for chunk in range(max(0, H - 1), NCH):
        pages_pass(chunk)
    while projected < Z - 1:
        project(projected)
        projected += 1
    project(0)
    while passed < Z:
        if passed == 6:
            far_pass()
        wx_pass(passed)
        passed += 1
    for d in range(2):
        arrived(rp_half(z + H, d), mids.at[2 + d], midr.at[2 + d], up_z)
    for k in range(1, Z - 1):
        arrived(rp_of(zmod(2 * z - z_of(k))), pjs.at[k - 1], pjr.at[k - 1], up_z)

    eye = (iota((SPAN, SPAN), 0) == iota((SPAN, SPAN), 1)).astype(BF16)
    for q_ in range(REQ):
        def place(j, carry, q_=q_):
            pt[j] = rp[places[j, q_]]
            return carry

        lax.fori_loop(0, 2 * HEADS, place, 0, unroll=8)
        rows = slice(q_ * SPAN, (q_ + 1) * SPAN)
        g = a0[rows, :] + a1[rows, :] * dot_nt(eye, pt[...].reshape(WIDTH, SPAN))
        scale = lax.rsqrt(jnp.mean(g * g, axis=-1, keepdims=True) + 1e-05)
        hid[rows, :] = (g * scale * gain[...]).astype(BF16)

    for k in range(Z):
        arrived(w_rows(x + 2, z_of(k), 0, 32), wfs.at[0, k], wfr.at[0, k], right_x)
        arrived(w_rows(x + 2, z_of(k), 32, 32), wfs.at[1, k], wfr.at[1, k], left_x)

    cols = out_ref.shape[1]

    def product(block):
        weights = wt[pl.ds(pl.multiple_of(block * cols, cols), cols), :]
        return dot_nt(hid[...], weights)

    if T == 1:
        out_ref[...] = product(0).astype(BF16)
    else:
        offsets = (2, 1, Y - 1, 0)

        def block_of(k, core):
            return lax.rem(y + offsets[k], Y) * 2 + core

        def give(k):
            xsend[k] = product(block_of(k, 1 - c)).astype(BF16)
            send(xsend.at[k], xrecv.at[k], coresem_s.at[k], coresem_r.at[k], other)

        def both(k):
            if k < 3:
                give(k + 1)
            mine = product(block_of(k, c))
            arrived(xrecv.at[k], coresem_s.at[k], coresem_r.at[k], other)
            return mine + xrecv[k].astype(F32)

        half = out_ref.shape[0] // 2
        lo, hi = pl.ds(0, half), pl.ds(half, half)
        give(0)
        ysend[0] = both(0).astype(BF16)
        send(ysend.at[0, lo], yrecv.at[0], ys_s.at[0], ys_r.at[0], y_up)
        send(ysend.at[0, hi], yrecv.at[1], ys_s.at[1], ys_r.at[1], y_down)
        up = both(1)
        ysend[1, hi] = up[half:].astype(BF16)
        send(ysend.at[1, hi], yrecv.at[2], ys_s.at[2], ys_r.at[2], y_up)
        down = both(2)
        ysend[2, lo] = down[:half].astype(BF16)
        send(ysend.at[2, lo], yrecv.at[3], ys_s.at[3], ys_r.at[3], y_down)
        arrived(yrecv.at[0], ys_s.at[0], ys_r.at[0], y_up)
        ysend[1, lo] = (up[:half] + yrecv[0].astype(F32)).astype(BF16)
        send(ysend.at[1, lo], yrecv.at[4], ys_s.at[4], ys_r.at[4], y_up)
        arrived(yrecv.at[1], ys_s.at[1], ys_r.at[1], y_down)
        ysend[2, hi] = (down[half:] + yrecv[1].astype(F32)).astype(BF16)
        send(ysend.at[2, hi], yrecv.at[5], ys_s.at[5], ys_r.at[5], y_down)
        own = both(3)
        for k in range(2, 6):
            arrived(yrecv.at[k], ys_s.at[k], ys_r.at[k], (y_up, y_down)[k % 2])
        low = own[:half] + yrecv[4].astype(F32) + yrecv[3].astype(F32)
        high = own[half:] + yrecv[2].astype(F32) + yrecv[5].astype(F32)
        out_ref[lo, :] = low.astype(BF16)
        out_ref[hi, :] = high.astype(BF16)

    for copy in sends:
        copy.wait_send()


def per_device(
    suffix_x, suffix_z, suffix_b, suffix_c, suffix_dt, missed_x, missed_b, missed_dt,
    dt_bias, a_log, skip_weight_per_head, norm_gain, out_weight, cache_pages,
    hit_holder, hit_slot, missed,
):
    R = lax.axis_size("replica")
    T = lax.axis_size("tensor")
    Z = R // X
    H = Z // 2
    smem = pl.BlockSpec(memory_space=pltpu.SMEM)
    vmem = pl.BlockSpec(memory_space=pltpu.VMEM)
    hbm = pl.BlockSpec(memory_space=pl.ANY)
    tokens = REQ * SPAN
    cols = out_weight.shape[1] * R // T
    V = pltpu.VMEM
    D = pltpu.SemaphoreType.DMA
    return pl.pallas_call(
        functools.partial(kernel, Z, T),
        out_shape=jax.ShapeDtypeStruct((tokens, cols), BF16),
        in_specs=[smem] * 4 + [vmem] * 5 + [hbm] * 3 + [vmem] + [hbm] * 2 + [vmem] * 2,
        out_specs=vmem,
        scratch_shapes=[
            V((tokens, WIDTH), BF16),
            V((tokens, WIDTH), BF16),
            V((tokens, N), BF16),
            V((MISS * tokens, WIDTH), BF16),
            V((MISS * tokens, N), BF16),
            D((5,)),
            pltpu.SMEM((16, 2 * R), jnp.int32),
            pltpu.SMEM((PAGES, 2 * R), jnp.int32),
            V((16, 2 * R), jnp.int32),
            V((PAGES, 2 * R), jnp.int32),
            D((2,)),
            V((R * 64, WIDTH), BF16),
            V((Z, tokens, N), BF16),
            V((3, Z, 2 * ROWS, N), BF16),
            V((4, Z, 2 * ROWS, N), BF16),
            V((2, H, 2 * ROWS, N), BF16),
            V((Z - 1, 2 * X, ROWS, SPAN), BF16),
            V((Z * 2 * X, ROWS, SPAN), BF16),
            V((2 * HEADS, ROWS, SPAN), BF16),
            V((tokens, WIDTH), F32),
            V((tokens, WIDTH), F32),
            V((MISS * SPAN, WIDTH), BF16),
            V((6, SPAN, SPAN), F32),
            V((8, WIDTH), F32),
            V((tokens, WIDTH), BF16),
            V((2, X, ROWS, SPAN), BF16),
            D((4,)), D((4,)),
            D((2, H)), D((2, H)), D((2, H)), D((2, H)),
            D((2, Z)), D((2, Z)), D((2, Z)), D((2, Z)),
            D((NCH, 6)), D((NCH, 6)), D((Z - 1,)), D((Z - 1,)),
            V((4, tokens, cols), BF16),
            V((4, tokens, cols), BF16),
            V((3, tokens, cols), BF16),
            V((6, tokens // 2, cols), BF16),
            D((4,)), D((4,)), D((6,)), D((6,)),
        ],
        compiler_params=pltpu.CompilerParams(
            collective_id=0, has_side_effects=True, vmem_limit_bytes=58 * 1024 * 1024
        ),
        cost_estimate=pl.CostEstimate(
            flops=4 * 10**9, bytes_accessed=8 * 10**6, transcendentals=10**6
        ),
    )(
        missed, dt_bias, a_log, skip_weight_per_head,
        hit_holder[0].transpose(1, 2, 0), hit_slot[0].T, suffix_dt.T, missed_dt.T, norm_gain[None],
        suffix_x, suffix_z, suffix_b, suffix_c, missed_x, missed_b, out_weight.T, cache_pages,
    )


def solution(mesh):
    in_specs = (
        P("replica", "tensor"),
        P("replica", "tensor"),
        P("replica", "tensor"),
        P("replica", "tensor"),
        P("replica", "tensor"),
        P("replica", "tensor"),
        P("replica", "tensor"),
        P("replica", "tensor"),
        P("tensor"),
        P("tensor"),
        P("tensor"),
        P("tensor"),
        P("tensor", "replica"),
        P("replica", "tensor", None, None),
        P("tensor", None, None, None),
        P("tensor", None, None),
        P("replica"),
    )
    return jax.shard_map(
        per_device, mesh=mesh, in_specs=in_specs, out_specs=P("replica", "tensor"), check_vma=False
    )
```
